32 devices in a mesh: sec: 4 (over y, core), op: 8 (over z, x).
Axes of the slice: x: 2, y: 2, z: 4, core: 2. Of those that a mesh axis runs over, the one named last changes fastest.
Arguments:
- psi: bfloat16 [8, 256, 256], P('sec', 'op'), may hold values from -6 to 6
- left_ops: bfloat16 [256, 256, 256], P(('sec', 'op')), may hold values from -0.0234375 to 0.0234375
- right_ops: bfloat16 [256, 256, 256], P(('sec', 'op')), may hold values from -0.375 to 0.375
- send_list: int32 [4, 8, 4, 1], replicated, may hold values from 0 to 7, as said below
- term_slot: int32 [2048], P(('sec', 'op')), may hold values from 0 to 3
- term_out: int32 [2048], P(('sec', 'op')), may hold values from 0 to 1
- left_pick: int32 [2048], P(('sec', 'op')), may hold values from 0 to 7
- right_pick: int32 [2048], P(('sec', 'op')), may hold values from 0 to 7
Outputs:
- h_psi: float32 [8, 256, 256], P('sec', 'op')
The draws below stay inside these ranges and needn't reach their ends.
Inputs may be any that keep to these rules, and one draw needn't show every extreme that they name: `send_list`: entry [s, o, d, c] is a sector held by index s of sec, between 2 * s and 2 * s + 1; the 1 entries of one s, o, d are distinct.
All inputs are finite; a program needn't handle non-finite values.
Results may differ from the reference program's by a relative error of at most 0.0041.
Values may be sent and summed in bfloat16 or wider, within the bound.
No kernel may reach another device: no remote copies, remote signals or barrier semaphores. Data moves between devices by JAX's collectives and lax.ppermute only.
A program may use at most 64 MiB of HBM per device.

```python
import jax
import jax.numpy as jnp
from jax import lax

B = 256
SEC_DEV = 2
CAP = 1
OPS_DEV = 8
TERM_DEV = 64
NSEC = 8
TERMS = 2048
OPS_TOTAL = 256
N_SEC = 4
N_OP = 8


def draw_send_list(key, part):
    scores = jax.random.randint(key, (N_SEC, N_OP, N_SEC, SEC_DEV), 0, 1 << 20)
    scores = scores * SEC_DEV + jnp.arange(SEC_DEV, dtype=jnp.int32)
    picked = jnp.argsort(scores, axis=-1)[..., :CAP]
    base = (jnp.arange(N_SEC, dtype=jnp.int32) * SEC_DEV)[:, None, None, None]
    return (picked + base).astype(jnp.int32)


def set_ends(result, own_key, low, largest):
    index_at = [jax.random.randint(jax.random.fold_in(own_key, axis), (), 0, length) for axis, length in enumerate(result.shape)]
    widest = result.shape.index(max(result.shape))
    neighbour = index_at[:widest] + [(index_at[widest] + 1) % result.shape[widest]] + index_at[widest + 1:]
    return result.at[tuple(index_at)].set(low).at[tuple(neighbour)].set(largest)


def block_levels(own_key, dims, cuts, least, high):
    factor_of, own = 1.0, jax.random.fold_in(own_key, 6)
    for position, blocks in cuts:
        heights = jnp.exp(jax.random.uniform(jax.random.fold_in(own, position), (blocks,), jnp.float32, least / len(cuts), high / len(cuts)))
        factor_of = factor_of * jnp.repeat(heights, dims[position] // blocks).reshape([-1 if axis == position else 1 for axis in range(len(dims))])
    return factor_of


def noise(own_key, extent, width, bound, pieces=(), kind=jnp.bfloat16):
    array = width * jax.random.normal(own_key, extent, jnp.float32)
    if pieces:
        array = array * block_levels(own_key, extent, pieces, -0.22, 0.18)
    return jnp.clip(array, -bound, bound).astype(kind)


def setup_inputs(seed: int = 0) -> dict:
    key_list = jax.random.split(jax.random.key(seed), 9)
    return {
        "psi": noise(key_list[0], (NSEC, B, B), 1.0, 6.0, ((0, 4), (1, 8))),
        "left_ops": noise(key_list[1], (OPS_TOTAL, B, B), (B * TERM_DEV * N_OP // SEC_DEV) ** -0.5, 0.0234375, ((0, 32),)),
        "right_ops": noise(key_list[2], (OPS_TOTAL, B, B), B ** -0.5, 0.375, ((0, 32),)),
        "send_list": draw_send_list(jax.random.fold_in(key_list[8], 71), 0),
        "term_slot": set_ends(jax.random.randint(key_list[4], (TERMS,), 0, N_SEC * CAP), jax.random.fold_in(key_list[4], 1), 0, (N_SEC * CAP) - 1).astype(jnp.int32),
        "term_out": set_ends(jax.random.randint(key_list[5], (TERMS,), 0, SEC_DEV), jax.random.fold_in(key_list[5], 1), 0, SEC_DEV - 1).astype(jnp.int32),
        "left_pick": set_ends(jax.random.randint(key_list[6], (TERMS,), 0, OPS_DEV), jax.random.fold_in(key_list[6], 1), 0, OPS_DEV - 1).astype(jnp.int32),
        "right_pick": set_ends(jax.random.randint(key_list[7], (TERMS,), 0, OPS_DEV), jax.random.fold_in(key_list[7], 1), 0, OPS_DEV - 1).astype(jnp.int32),
    }


def reference(psi, left_ops, right_ops, send_list, term_slot, term_out, left_pick, right_pick):
    devices = N_SEC * N_OP
    owner = jnp.arange(TERMS, dtype=jnp.int32) // TERM_DEV
    sec_index = owner // N_OP
    op_index = owner % N_OP
    source = term_slot // CAP
    column = term_slot % CAP
    sector_in = send_list[source, op_index, sec_index, column]
    sector_out = sec_index * SEC_DEV + term_out
    left_index = owner * OPS_DEV + left_pick
    right_index = owner * OPS_DEV + right_pick

    def one_device(total, items):
        s_in, s_out, l_idx, r_idx = items
        left = left_ops[l_idx].astype(jnp.float32)
        block = psi[s_in].astype(jnp.float32)
        right = right_ops[r_idx].astype(jnp.float32)
        half = jnp.einsum("kab,kbc->kac", left, block).astype(jnp.bfloat16)
        half = lax.optimization_barrier(half).astype(jnp.float32)
        term = jnp.einsum("kac,kdc->kad", half, right).astype(jnp.bfloat16)
        term = lax.optimization_barrier(term).astype(jnp.float32)
        return total.at[s_out].add(term), None

    shaped = (sector_in.reshape(devices, TERM_DEV), sector_out.reshape(devices, TERM_DEV),
              left_index.reshape(devices, TERM_DEV), right_index.reshape(devices, TERM_DEV))
    start = jnp.zeros((NSEC, B, B), jnp.float32)
    h_psi, unused = lax.scan(one_device, start, shaped)
    return h_psi
```

```python
import functools

import jax
import jax.numpy as jnp
from jax import lax
from jax.experimental import pallas as pl
from jax.experimental.pallas import tpu as pltpu
from jax.sharding import PartitionSpec as P

CHUNK = 16
VMEM = pl.BlockSpec(memory_space=pltpu.VMEM)
SMEM = pl.BlockSpec(memory_space=pltpu.SMEM)
NT = (((1,), (1,)), ((), ()))


def pack_kernel(cap, held, place_ref, listed_ref, psi_ref, out_ref):
    my_sec = place_ref[0]
    n_sec, n_op = out_ref.shape[0], out_ref.shape[1]
    for d in range(n_sec):
        for o in range(n_op):
            for c in range(cap):
                sector = listed_ref[((my_sec * n_op + o) * n_sec + d) * cap + c] - my_sec * held
                out_ref[d, o, c] = psi_ref[sector]


def pack(psi, send_list):
    held, rows, width = psi.shape
    n_sec, n_op, _, cap = send_list.shape
    place = lax.axis_index("sec").astype(jnp.int32).reshape(1)
    return pl.pallas_call(
        functools.partial(pack_kernel, cap, held),
        out_shape=jax.ShapeDtypeStruct((n_sec, n_op, cap, rows, width), psi.dtype),
        in_specs=[SMEM, SMEM, VMEM],
        out_specs=VMEM,
    )(place, send_list.reshape(-1), psi)


def terms_kernel(split, slot_ref, out_id_ref, left_id_ref, right_id_ref, left_ref, right_ref, table_ref,
                 out_ref, half_ref, weight_ref, sum_ref):
    n_left, width = left_ref.shape[0], left_ref.shape[1]
    n_right = right_ref.shape[0]
    n_slot = table_ref.shape[0]
    n_pair = n_left * n_slot
    held = sum_ref.shape[0] // width
    n_cell = held * n_right
    chunks = width // CHUNK

    cell = out_id_ref[...] * n_right + right_id_ref[...]
    pair = slot_ref[...] * n_left + left_id_ref[...]
    n_term = cell.shape[1]
    row_cell = lax.broadcasted_iota(jnp.int32, (n_cell * CHUNK, n_term), 0) // CHUNK
    row_pair = lax.broadcasted_iota(jnp.int32, (n_pair * CHUNK, n_term), 0) // CHUNK
    in_cell = jnp.where(row_cell == cell, 1.0, 0.0).astype(jnp.bfloat16)
    in_pair = jnp.where(row_pair == pair, 1.0, 0.0).astype(jnp.bfloat16)
    count = lax.dot_general(in_cell, in_pair, NT, preferred_element_type=jnp.float32)
    a = lax.broadcasted_iota(jnp.int32, count.shape, 0) % CHUNK
    b = lax.broadcasted_iota(jnp.int32, count.shape, 1) % CHUNK
    weight_ref[...] = jnp.where(a == b, count, 0.0).astype(jnp.bfloat16)

    for s in range(n_slot):
        for l in range(n_left):
            half = jnp.dot(left_ref[l], table_ref[s], preferred_element_type=jnp.float32).astype(jnp.bfloat16)
            p = s * n_left + l
            for m in range(chunks):
                half_ref[m, p * CHUNK:(p + 1) * CHUNK, :] = half[m * CHUNK:(m + 1) * CHUNK, :]

    for m in range(chunks):
        total = jnp.dot(weight_ref[...], half_ref[m], preferred_element_type=jnp.float32).astype(jnp.bfloat16)
        for j in range(held):
            for r in range(n_right):
                p = j * n_right + r
                sum_ref[j * width + m * CHUNK:j * width + (m + 1) * CHUNK, r * width:(r + 1) * width] = (
                    total[p * CHUNK:(p + 1) * CHUNK, :])

    for j in range(held):
        acc = jnp.zeros((width, width), jnp.float32)
        for r in range(n_right):
            acc = acc + lax.dot_general(
                sum_ref[j * width:(j + 1) * width, r * width:(r + 1) * width], right_ref[r], NT,
                preferred_element_type=jnp.float32)
        acc = acc.astype(out_ref.dtype)
        if split:
            n_op, rows = out_ref.shape[0], out_ref.shape[2]
            for o in range(n_op):
                out_ref[o, j] = acc[o * rows:(o + 1) * rows, :]
        else:
            out_ref[j] = acc


def terms(table, left_ops, right_ops, term_slot, term_out, left_pick, right_pick, held, n_op):
    n_slot, width = table.shape[0], table.shape[1]
    n_left, n_right = left_ops.shape[0], right_ops.shape[0]
    n_term = term_slot.shape[0]
    rows = width // n_op
    split = rows % 16 == 0
    shape = (n_op, held, rows, width) if split else (held, width, width)
    ids = [x.reshape(1, n_term) for x in (term_slot, term_out, left_pick, right_pick)]
    out = pl.pallas_call(
        functools.partial(terms_kernel, split),
        out_shape=jax.ShapeDtypeStruct(shape, jnp.bfloat16),
        in_specs=[VMEM] * 7,
        out_specs=VMEM,
        scratch_shapes=[
            pltpu.VMEM((width // CHUNK, n_slot * n_left * CHUNK, width), jnp.bfloat16),
            pltpu.VMEM((held * n_right * CHUNK, n_slot * n_left * CHUNK), jnp.bfloat16),
            pltpu.VMEM((held * width, n_right * width), jnp.bfloat16),
        ],
        compiler_params=pltpu.CompilerParams(vmem_limit_bytes=48 * 1024 * 1024),
        cost_estimate=pl.CostEstimate(flops=6 * 10**9, bytes_accessed=4 * 10**6, transcendentals=0),
    )(*ids, left_ops, right_ops, table)
    if not split:
        out = out.reshape(held, n_op, rows, width).transpose(1, 0, 2, 3)
    return out


def shards(psi, left_ops, right_ops, send_list, term_slot, term_out, left_pick, right_pick):
    held, rows, width = psi.shape
    n_sec, n_op, _, cap = send_list.shape
    packed = pack(psi, send_list).reshape(n_sec * n_op, cap, rows, width)
    got = lax.all_to_all(packed, ("sec", "op"), 0, 0, tiled=True)
    table = got.reshape(n_sec, n_op, cap, rows, width).transpose(0, 2, 1, 3, 4).reshape(n_sec * cap, width, width)
    partial_sum = terms(table, left_ops, right_ops, term_slot, term_out, left_pick, right_pick, held, n_op)
    parts = lax.all_to_all(partial_sum, "op", 0, 0, tiled=True)
    return jnp.sum(parts.astype(jnp.float32), axis=0)


def solution(mesh):
    in_specs = (
        P("sec", "op", None),
        P(("sec", "op"), None, None),
        P(("sec", "op"), None, None),
        P(),
        P(("sec", "op")),
        P(("sec", "op")),
        P(("sec", "op")),
        P(("sec", "op")),
    )
    out_specs = P("sec", "op", None)
    return jax.shard_map(shards, mesh=mesh, in_specs=in_specs, out_specs=out_specs, check_vma=False)
```

```python
import functools

import jax
import jax.numpy as jnp
from jax import lax
from jax.experimental import pallas as pl
from jax.experimental.pallas import tpu as pltpu
from jax.sharding import PartitionSpec as P

CHUNK = 8
VMEM = pl.BlockSpec(memory_space=pltpu.VMEM)
SMEM = pl.BlockSpec(memory_space=pltpu.SMEM)
ANY = pl.BlockSpec(memory_space=pl.ANY)
NT = (((1,), (1,)), ((), ()))
BF16 = jnp.bfloat16


def choose_kernel(held, place_ref, listed_ref, choice_ref, side_ref):
    my_sec, my_half = place_ref[0], place_ref[1]
    n_sec, half_op, cap = choice_ref.shape[:3]
    for d in range(n_sec):
        for q in range(half_op):
            for c in range(cap):
                choice = listed_ref[my_sec, d, c, my_half * half_op + q] - my_sec * held
                choice_ref[d, q, c] = jnp.full(choice_ref.shape[3:], choice.astype(jnp.float32)).astype(BF16)
    side_ref[...] = jnp.full(side_ref.shape, my_half.astype(jnp.float32)).astype(BF16)


def choose(send_list, held, rows, width):
    n_sec, n_op, _, cap = send_list.shape
    place = jnp.stack([lax.axis_index("sec"), lax.div(lax.axis_index("op"), n_op // 2)]).astype(jnp.int32)
    return pl.pallas_call(
        functools.partial(choose_kernel, held),
        out_shape=[
            jax.ShapeDtypeStruct((n_sec, n_op // 2, cap, rows, width), BF16),
            jax.ShapeDtypeStruct((rows, width), BF16),
        ],
        in_specs=[SMEM, SMEM],
        out_specs=[VMEM, VMEM],
        compiler_params=pltpu.CompilerParams(vmem_limit_bytes=4 * 1024 * 1024),
        cost_estimate=pl.CostEstimate(flops=10**6, bytes_accessed=2 * 10**6, transcendentals=0),
    )(place, send_list.transpose(0, 2, 3, 1))


def weight_kernel(n_left, n_right, slot_hbm, out_id_hbm, left_id_hbm, right_id_hbm, weight_ref, ids_ref, sems):
    n_pair, n_cell = weight_ref.shape[1] // CHUNK, weight_ref.shape[0] // CHUNK
    copies = [pltpu.make_async_copy(x, ids_ref.at[i], sems.at[i])
              for i, x in enumerate((slot_hbm, out_id_hbm, left_id_hbm, right_id_hbm))]
    for copy in copies:
        copy.start()
    for copy in copies:
        copy.wait()

    cell = ids_ref[1] * n_right + ids_ref[3]
    pair = ids_ref[0] * n_left + ids_ref[2]
    n_term = cell.shape[1]
    row_cell = lax.broadcasted_iota(jnp.int32, (n_cell * CHUNK, n_term), 0) // CHUNK
    row_pair = lax.broadcasted_iota(jnp.int32, (n_pair * CHUNK, n_term), 0) // CHUNK
    in_cell = jnp.where(row_cell == cell, 1.0, 0.0).astype(BF16)
    in_pair = jnp.where(row_pair == pair, 1.0, 0.0).astype(BF16)
    count = lax.dot_general(in_cell, in_pair, NT, preferred_element_type=jnp.float32)
    a = lax.broadcasted_iota(jnp.int32, count.shape, 0) % CHUNK
    b = lax.broadcasted_iota(jnp.int32, count.shape, 1) % CHUNK
    weight_ref[...] = jnp.where(a == b, count, 0.0).astype(BF16)


def weights(n_slot, n_left, n_right, held, term_slot, term_out, left_pick, right_pick):
    n_pair, n_cell = n_slot * n_left, held * n_right
    n_term = term_slot.shape[0]
    ids = [x.reshape(1, n_term) for x in (term_slot, term_out, left_pick, right_pick)]
    return pl.pallas_call(
        functools.partial(weight_kernel, n_left, n_right),
        out_shape=jax.ShapeDtypeStruct((n_cell * CHUNK, n_pair * CHUNK), BF16),
        in_specs=[ANY] * 4,
        out_specs=VMEM,
        scratch_shapes=[pltpu.VMEM((4, 1, n_term), jnp.int32), pltpu.SemaphoreType.DMA((4,))],
        compiler_params=pltpu.CompilerParams(vmem_limit_bytes=8 * 1024 * 1024),
        cost_estimate=pl.CostEstimate(flops=10**9, bytes_accessed=8 * 10**6, transcendentals=0),
    )(*ids)


def pack_kernel(choice_ref, side_ref, near_ref, far_ref, out_ref):
    n_sec, half_op, cap = choice_ref.shape[:3]
    low = side_ref[...] == 0
    pairs = [(jnp.where(low, near_ref[t], far_ref[t]), jnp.where(low, far_ref[t], near_ref[t]))
             for t in range(near_ref.shape[0])]
    for d in range(n_sec):
        for q in range(half_op):
            for c in range(cap):
                choice = choice_ref[d, q, c]
                first, second = pairs[0]
                for t in range(1, len(pairs)):
                    first = jnp.where(choice == t, pairs[t][0], first)
                    second = jnp.where(choice == t, pairs[t][1], second)
                out_ref[d, q, 0, c] = first
                out_ref[d, q, 1, c] = second


def pack(near, far, choice, side):
    n_sec, half_op, cap, rows, width = choice.shape
    return pl.pallas_call(
        pack_kernel,
        out_shape=jax.ShapeDtypeStruct((n_sec, half_op, 2, cap, rows, width), near.dtype),
        in_specs=[VMEM] * 4,
        out_specs=VMEM,
        compiler_params=pltpu.CompilerParams(vmem_limit_bytes=4 * 1024 * 1024),
        cost_estimate=pl.CostEstimate(flops=10**6, bytes_accessed=2 * 10**6, transcendentals=0),
    )(choice, side, near, far)


def terms_kernel(split, left_ref, right_ref, weight_ref, table_ref, out_ref, half_ref, sum_ref):
    n_left, width = left_ref.shape[0], left_ref.shape[1]
    n_right = right_ref.shape[0]
    n_slot = table_ref.shape[0]
    held = sum_ref.shape[0] // width
    chunks = width // CHUNK

    for s in range(n_slot):
        block = [table_ref[s, q, h] for h in range(table_ref.shape[2]) for q in range(table_ref.shape[1])]
        block = jnp.concatenate(block, axis=0) if len(block) > 1 else block[0]
        for l in range(0, n_left, 2):
            two = [jnp.dot(left_ref[l + i], block, preferred_element_type=jnp.float32) for i in range(2)]
            p = s * n_left + l
            for m in range(chunks):
                piece = jnp.concatenate([x[m * CHUNK:(m + 1) * CHUNK, :] for x in two], axis=0)
                half_ref[m, p * CHUNK:(p + 2) * CHUNK, :] = piece.astype(BF16)

    for m in range(0, chunks, 2):
        two = [jnp.dot(weight_ref[...], half_ref[m + i], preferred_element_type=jnp.float32) for i in range(2)]
        for j in range(held):
            for r in range(n_right):
                p = j * n_right + r
                piece = jnp.concatenate([x[p * CHUNK:(p + 1) * CHUNK, :] for x in two], axis=0)
                sum_ref[j * width + m * CHUNK:j * width + (m + 2) * CHUNK, r * width:(r + 1) * width] = piece.astype(BF16)

    for j in range(held):
        acc = None
        for r in range(n_right):
            part = lax.dot_general(
                sum_ref[j * width:(j + 1) * width, r * width:(r + 1) * width], right_ref[r], NT,
                preferred_element_type=jnp.float32)
            acc = part if acc is None else acc + part
        acc = acc.astype(out_ref.dtype)
        if split:
            n_op, rows = out_ref.shape[0], out_ref.shape[2]
            for o in range(n_op):
                out_ref[o, j] = acc[o * rows:(o + 1) * rows, :]
        else:
            out_ref[j] = acc


def terms(table, left, right, weight, held, n_op):
    n_slot, width = table.shape[0], table.shape[-1]
    n_left, n_right = left.shape[0], right.shape[0]
    rows = width // n_op
    split = rows % 16 == 0
    shape = (n_op, held, rows, width) if split else (held, width, width)
    n_pair, n_cell = n_slot * n_left, held * n_right
    blocks = n_pair + n_cell + n_left + n_right + n_slot + 4 * held
    out = pl.pallas_call(
        functools.partial(terms_kernel, split),
        out_shape=jax.ShapeDtypeStruct(shape, BF16),
        in_specs=[VMEM] * 4,
        out_specs=VMEM,
        scratch_shapes=[
            pltpu.VMEM((width // CHUNK, n_pair * CHUNK, width), BF16),
            pltpu.VMEM((held * width, n_right * width), BF16),
        ],
        compiler_params=pltpu.CompilerParams(vmem_limit_bytes=2 * width * width * blocks + 16 * 1024 * 1024),
        cost_estimate=pl.CostEstimate(flops=5 * 10**9, bytes_accessed=4 * 10**6, transcendentals=0),
    )(left, right, weight, table)
    if not split:
        out = out.reshape(held, n_op, rows, width).transpose(1, 0, 2, 3)
    return out


def shards(psi, left_ops, right_ops, send_list, term_slot, term_out, left_pick, right_pick):
    held, rows, width = psi.shape
    n_sec, n_op, _, cap = send_list.shape
    half_op = n_op // 2
    far = lax.ppermute(psi, "op", [(o, o ^ half_op) for o in range(n_op)])
    choice, side = choose(send_list, held, rows, psi.shape[2])
    weight = weights(
        n_sec * cap, left_ops.shape[0], right_ops.shape[0], held, term_slot, term_out, left_pick, right_pick)
    packed = pack(psi, far, choice, side).reshape(n_sec * half_op, 2, cap, rows, width)
    groups = [[s * n_op + h * half_op + q for s in range(n_sec) for q in range(half_op)] for h in range(2)]
    got = lax.all_to_all(packed, ("sec", "op"), 0, 0, tiled=True, axis_index_groups=groups)
    got = got.reshape(n_sec, half_op, 2, cap, rows, width).transpose(0, 3, 1, 2, 4, 5)
    table = got.reshape(n_sec * cap, half_op, 2, rows, width)
    if rows % 16:
        table = table.transpose(0, 2, 1, 3, 4).reshape(n_sec * cap, 1, 1, width, width)
    partial_sum = terms(table, left_ops, right_ops, weight, held, n_op)
    parts = lax.all_to_all(partial_sum, "op", 0, 0, tiled=True)
    return jnp.sum(parts.astype(jnp.float32), axis=0)


def solution(mesh):
    in_specs = (
        P("sec", "op", None),
        P(("sec", "op"), None, None),
        P(("sec", "op"), None, None),
        P(),
        P(("sec", "op")),
        P(("sec", "op")),
        P(("sec", "op")),
        P(("sec", "op")),
    )
    out_specs = P("sec", "op", None)
    return jax.shard_map(shards, mesh=mesh, in_specs=in_specs, out_specs=out_specs, check_vma=False)
```

```python
import functools

import jax
import jax.numpy as jnp
from jax import lax
from jax.experimental import pallas as pl
from jax.experimental.pallas import tpu as pltpu
from jax.sharding import PartitionSpec as P

CHUNK = 8
VMEM = pl.BlockSpec(memory_space=pltpu.VMEM)
SMEM = pl.BlockSpec(memory_space=pltpu.SMEM)
ANY = pl.BlockSpec(memory_space=pl.ANY)
NT = (((1,), (1,)), ((), ()))
BF16 = jnp.bfloat16


def choose_kernel(listed_ref, psi_ref, near_ref, choice_ref):
    held = psi_ref.shape[0]
    near_ref[...] = psi_ref[...]
    me, my_op = lax.axis_index("sec"), lax.axis_index("op")
    core = lax.rem(me, 2)
    for t in range(2):
        for y in range(choice_ref.shape[1]):
            source = 2 * y + core
            choice = listed_ref[source, jnp.bitwise_xor(me, t), 0, my_op] - source * held
            choice_ref[t, y] = jnp.full(choice_ref.shape[2:], choice.astype(jnp.float32)).astype(BF16)


def choose(send_list, psi):
    n_sec = send_list.shape[0]
    return pl.pallas_call(
        choose_kernel,
        out_shape=[
            jax.ShapeDtypeStruct(psi.shape, psi.dtype),
            jax.ShapeDtypeStruct((2, n_sec // 2) + psi.shape[1:], BF16),
        ],
        in_specs=[SMEM, VMEM],
        out_specs=[VMEM, VMEM],
        compiler_params=pltpu.CompilerParams(vmem_limit_bytes=4 * 1024 * 1024),
        cost_estimate=pl.CostEstimate(flops=10**6, bytes_accessed=10**6, transcendentals=0),
    )(send_list.transpose(0, 2, 3, 1), psi)


def weight_kernel(n_left, n_right, slot_hbm, out_id_hbm, left_id_hbm, right_id_hbm, weight_ref, ids_ref, sems):
    n_pair, n_cell = weight_ref.shape[1] // CHUNK, weight_ref.shape[0] // CHUNK
    copies = [pltpu.make_async_copy(x, ids_ref.at[i], sems.at[i])
              for i, x in enumerate((slot_hbm, out_id_hbm, left_id_hbm, right_id_hbm))]
    for copy in copies:
        copy.start()
    for copy in copies:
        copy.wait()

    cell = ids_ref[1] * n_right + ids_ref[3]
    slot = ids_ref[0]
    other = jnp.bitwise_xor(lax.rem(slot, 2), lax.rem(lax.axis_index("sec"), 2))
    pair = (other * (n_pair // (2 * n_left)) + lax.div(slot, 2)) * n_left + ids_ref[2]
    n_term = cell.shape[1]
    row_cell = lax.broadcasted_iota(jnp.int32, (n_cell * CHUNK, n_term), 0) // CHUNK
    row_pair = lax.broadcasted_iota(jnp.int32, (n_pair * CHUNK, n_term), 0) // CHUNK
    in_cell = jnp.where(row_cell == cell, 1.0, 0.0).astype(BF16)
    in_pair = jnp.where(row_pair == pair, 1.0, 0.0).astype(BF16)
    count = lax.dot_general(in_cell, in_pair, NT, preferred_element_type=jnp.float32)
    a = lax.broadcasted_iota(jnp.int32, count.shape, 0) % CHUNK
    b = lax.broadcasted_iota(jnp.int32, count.shape, 1) % CHUNK
    weight_ref[...] = jnp.where(a == b, count, 0.0).astype(BF16)


def weights(n_slot, n_left, n_right, held, term_slot, term_out, left_pick, right_pick):
    n_pair, n_cell = n_slot * n_left, held * n_right
    n_term = term_slot.shape[0]
    ids = [x.reshape(1, n_term) for x in (term_slot, term_out, left_pick, right_pick)]
    return pl.pallas_call(
        functools.partial(weight_kernel, n_left, n_right),
        out_shape=jax.ShapeDtypeStruct((n_cell * CHUNK, n_pair * CHUNK), BF16),
        in_specs=[ANY] * 4,
        out_specs=VMEM,
        scratch_shapes=[pltpu.VMEM((4, 1, n_term), jnp.int32), pltpu.SemaphoreType.DMA((4,))],
        compiler_params=pltpu.CompilerParams(vmem_limit_bytes=8 * 1024 * 1024),
        cost_estimate=pl.CostEstimate(flops=10**9, bytes_accessed=8 * 10**6, transcendentals=0),
    )(*ids)


def stack_kernel(*refs):
    for k, ref in enumerate(refs[:-1]):
        refs[-1][k] = ref[...]


def stack(blocks):
    return pl.pallas_call(
        stack_kernel,
        out_shape=jax.ShapeDtypeStruct((len(blocks),) + blocks[0].shape, blocks[0].dtype),
        in_specs=[VMEM] * len(blocks),
        out_specs=VMEM,
        compiler_params=pltpu.CompilerParams(vmem_limit_bytes=4 * 1024 * 1024),
        cost_estimate=pl.CostEstimate(flops=1, bytes_accessed=10**6, transcendentals=0),
    )(*blocks)


def split_kernel(n_lo, choice_ref, *refs):
    pieces, (keep_ref, give_ref) = refs[:-2], refs[-2:]
    n_hi, held = pieces[0].shape[:2]
    my_y = lax.div(lax.axis_index("sec"), 2)
    my_op = lax.axis_index("op")
    for q, piece in enumerate(pieces):
        y = jnp.bitwise_xor(my_y, q // n_lo)
        choices = [choice_ref[t, y] for t in range(2)]
        for k in range(n_hi):
            o = jnp.bitwise_xor(my_op, k * n_lo + q % n_lo)
            for choice, out_ref in zip(choices, (keep_ref, give_ref)):
                block = piece[k, 0]
                for i in range(1, held):
                    block = jnp.where(choice == i, piece[k, i], block)
                out_ref[y, o] = block


def split(choice, pieces, n_lo):
    n_hi, held, rows, width = pieces[0].shape
    out = jax.ShapeDtypeStruct((choice.shape[1], n_hi * n_lo, rows, width), BF16)
    return pl.pallas_call(
        functools.partial(split_kernel, n_lo),
        out_shape=[out, out],
        in_specs=[VMEM] * (1 + len(pieces)),
        out_specs=[VMEM] * 2,
        compiler_params=pltpu.CompilerParams(vmem_limit_bytes=8 * 1024 * 1024),
        cost_estimate=pl.CostEstimate(flops=10**6, bytes_accessed=2 * 10**6, transcendentals=0),
    )(choice, *pieces)


def halves(left_ref, table_ref, half_ref):
    n_left, width = left_ref.shape[0], left_ref.shape[1]
    for s in range(table_ref.shape[0]):
        for l in range(0, n_left, 2):
            two = [jnp.dot(left_ref[l + i], table_ref[s], preferred_element_type=jnp.float32) for i in range(2)]
            p = s * n_left + l
            for m in range(width // CHUNK):
                piece = jnp.concatenate([x[m * CHUNK:(m + 1) * CHUNK, :] for x in two], axis=0)
                half_ref[m, p * CHUNK:(p + 2) * CHUNK, :] = piece.astype(BF16)


def first_halves(table, left):
    n_slot, width, _ = table.shape
    n_left = left.shape[0]
    return pl.pallas_call(
        halves,
        out_shape=jax.ShapeDtypeStruct((width // CHUNK, n_slot * n_left * CHUNK, width), BF16),
        in_specs=[VMEM] * 2,
        out_specs=VMEM,
        compiler_params=pltpu.CompilerParams(vmem_limit_bytes=8 * 1024 * 1024),
        cost_estimate=pl.CostEstimate(flops=2 * n_slot * n_left * width**3, bytes_accessed=10**6, transcendentals=0),
    )(left, table)


def terms_kernel(split_rows, left_ref, right_ref, weight_ref, first_ref, table_ref, out_ref, half_ref, sum_ref):
    width, n_right = left_ref.shape[1], right_ref.shape[0]
    held = sum_ref.shape[0] // width
    chunks = width // CHUNK
    halves(left_ref, table_ref, half_ref)

    for m in range(0, chunks, 2):
        two = [jnp.dot(weight_ref[...], jnp.concatenate([first_ref[m + i], half_ref[m + i]], axis=0),
                       preferred_element_type=jnp.float32) for i in range(2)]
        for j in range(held):
            for r in range(n_right):
                p = j * n_right + r
                piece = jnp.concatenate([x[p * CHUNK:(p + 1) * CHUNK, :] for x in two], axis=0)
                sum_ref[j * width + m * CHUNK:j * width + (m + 2) * CHUNK, r * width:(r + 1) * width] = piece.astype(BF16)

    for j in range(held):
        acc = None
        for r in range(n_right):
            part = lax.dot_general(
                sum_ref[j * width:(j + 1) * width, r * width:(r + 1) * width], right_ref[r], NT,
                preferred_element_type=jnp.float32)
            acc = part if acc is None else acc + part
        acc = acc.astype(out_ref.dtype)
        if split_rows:
            n_op, rows = out_ref.shape[0], out_ref.shape[2]
            for o in range(n_op):
                out_ref[o, j] = acc[o * rows:(o + 1) * rows, :]
        else:
            out_ref[j] = acc


def terms(first, table, left, right, weight, held, n_op):
    n_slot, width, _ = table.shape
    n_left, n_right = left.shape[0], right.shape[0]
    rows = width // n_op
    split_rows = rows % 16 == 0
    shape = (n_op, held, rows, width) if split_rows else (held, width, width)
    n_pair, n_cell = n_slot * n_left, held * n_right
    blocks = n_pair + n_cell + n_left + n_right + n_slot + 4 * held
    out = pl.pallas_call(
        functools.partial(terms_kernel, split_rows),
        out_shape=jax.ShapeDtypeStruct(shape, BF16),
        in_specs=[VMEM] * 5,
        out_specs=VMEM,
        scratch_shapes=[
            pltpu.VMEM((width // CHUNK, n_pair * CHUNK, width), BF16),
            pltpu.VMEM((held * width, n_right * width), BF16),
        ],
        compiler_params=pltpu.CompilerParams(vmem_limit_bytes=2 * width * width * blocks + 12 * 1024 * 1024),
        cost_estimate=pl.CostEstimate(flops=3 * 10**9, bytes_accessed=4 * 10**6, transcendentals=0),
    )(left, right, weight, first, table)
    if not split_rows:
        out = out.reshape(held, n_op, rows, width).transpose(1, 0, 2, 3)
    return out


def shards(psi, left_ops, right_ops, send_list, term_slot, term_out, left_pick, right_pick):
    held, rows, width = psi.shape
    n_sec, n_op = send_list.shape[:2]
    n_lo = 2
    n_hi, n_y = n_op // n_lo, n_sec // 2

    def swap(x, sec_bits, op_bits):
        pairs = [(s * n_op + o, (s ^ sec_bits) * n_op + (o ^ op_bits)) for s in range(n_sec) for o in range(n_op)]
        return lax.ppermute(x, ("sec", "op"), pairs)

    near, choice = choose(send_list, psi)
    mine = stack([near] + [swap(psi, 0, k * n_lo) for k in range(1, n_hi)])
    pieces = [mine] + [swap(mine, 2 * (q // n_lo), q % n_lo) for q in range(1, n_y * n_lo)]
    weight = weights(n_sec, left_ops.shape[0], right_ops.shape[0], held, term_slot, term_out, left_pick, right_pick)
    choice, weight = lax.optimization_barrier((choice, weight))
    keep, give = (x.reshape(n_y, width, width) for x in split(choice, pieces, n_lo))
    got = swap(give, 1, 0)
    first = first_halves(keep, left_ops)
    partial_sum = terms(first, got, left_ops, right_ops, weight, held, n_op)
    parts = lax.all_to_all(partial_sum, "op", 0, 0, tiled=True)
    return jnp.sum(parts.astype(jnp.float32), axis=0)


def solution(mesh):
    in_specs = (
        P("sec", "op", None),
        P(("sec", "op"), None, None),
        P(("sec", "op"), None, None),
        P(),
        P(("sec", "op")),
        P(("sec", "op")),
        P(("sec", "op")),
        P(("sec", "op")),
    )
    out_specs = P("sec", "op", None)
    return jax.shard_map(shards, mesh=mesh, in_specs=in_specs, out_specs=out_specs, check_vma=False)
```

```python
import functools

import jax
import jax.numpy as jnp
from jax import lax
from jax.experimental import pallas as pl
from jax.experimental.pallas import tpu as pltpu
from jax.sharding import PartitionSpec as P

CHUNK = 8
VMEM = pl.BlockSpec(memory_space=pltpu.VMEM)
SMEM = pl.BlockSpec(memory_space=pltpu.SMEM)
ANY = pl.BlockSpec(memory_space=pl.ANY)
NT = (((1,), (1,)), ((), ()))
BF16 = jnp.bfloat16


def fetch_kernel(from_ref, to_ref, sem):
    copy = pltpu.make_async_copy(from_ref, to_ref, sem)
    copy.start()
    copy.wait()


def fetch(x):
    return pl.pallas_call(
        fetch_kernel,
        out_shape=jax.ShapeDtypeStruct(x.shape, x.dtype),
        in_specs=[ANY],
        out_specs=VMEM,
        scratch_shapes=[pltpu.SemaphoreType.DMA],
        compiler_params=pltpu.CompilerParams(vmem_limit_bytes=4 * 1024 * 1024),
        cost_estimate=pl.CostEstimate(flops=1, bytes_accessed=10**6, transcendentals=0),
    )(x)


def prepare_kernel(n_left, n_right, held, listed_ref, code_ref, choice_ref, weight_ref):
    n_pair, n_cell = weight_ref.shape[1] // CHUNK, weight_ref.shape[0] // CHUNK
    me, my_op = lax.axis_index("sec"), lax.axis_index("op")
    core = lax.rem(me, 2)
    for t in range(2):
        for y in range(choice_ref.shape[1]):
            source = 2 * y + core
            choice = listed_ref[source, jnp.bitwise_xor(me, t), 0, my_op] - source * held
            choice_ref[t, y] = jnp.full(choice_ref.shape[2:], choice.astype(jnp.float32)).astype(BF16)

    code = code_ref[...]
    cell, code = lax.rem(code, n_cell), lax.div(code, n_cell)
    left, slot = lax.rem(code, n_left), lax.div(code, n_left)
    other = jnp.bitwise_xor(lax.rem(slot, 2), core)
    pair = (other * (n_pair // (2 * n_left)) + lax.div(slot, 2)) * n_left + left
    n_term = cell.shape[1]
    row_cell = lax.broadcasted_iota(jnp.int32, (n_cell * CHUNK, n_term), 0) // CHUNK
    row_pair = lax.broadcasted_iota(jnp.int32, (n_pair * CHUNK, n_term), 0) // CHUNK
    in_cell = jnp.where(row_cell == cell, 1.0, 0.0).astype(BF16)
    in_pair = jnp.where(row_pair == pair, 1.0, 0.0).astype(BF16)
    count = lax.dot_general(in_cell, in_pair, NT, preferred_element_type=jnp.float32)
    a = lax.broadcasted_iota(jnp.int32, count.shape, 0) % CHUNK
    b = lax.broadcasted_iota(jnp.int32, count.shape, 1) % CHUNK
    weight_ref[...] = jnp.where(a == b, count, 0.0).astype(BF16)


def prepare(send_list, term_slot, term_out, left_pick, right_pick, held, rows, width, n_left, n_right):
    n_sec = send_list.shape[0]
    n_pair, n_cell = n_sec * n_left, held * n_right
    n_term = term_slot.shape[0]
    code = ((term_slot * n_left + left_pick) * held + term_out) * n_right + right_pick
    return pl.pallas_call(
        functools.partial(prepare_kernel, n_left, n_right, held),
        out_shape=[
            jax.ShapeDtypeStruct((2, n_sec // 2, rows, width), BF16),
            jax.ShapeDtypeStruct((n_cell * CHUNK, n_pair * CHUNK), BF16),
        ],
        in_specs=[SMEM, VMEM],
        out_specs=[VMEM] * 2,
        compiler_params=pltpu.CompilerParams(vmem_limit_bytes=8 * 1024 * 1024),
        cost_estimate=pl.CostEstimate(flops=10**9, bytes_accessed=4 * 10**6, transcendentals=0),
    )(send_list.transpose(0, 2, 3, 1), code.reshape(1, n_term))


def stack_kernel(order, *refs):
    for k, ref in zip(order, refs[:-1]):
        refs[-1][k] = ref[...]


def stack(blocks):
    first = next(iter(blocks.values()))
    return pl.pallas_call(
        functools.partial(stack_kernel, tuple(blocks)),
        out_shape=jax.ShapeDtypeStruct((len(blocks),) + first.shape, first.dtype),
        in_specs=[VMEM] * len(blocks),
        out_specs=VMEM,
        compiler_params=pltpu.CompilerParams(vmem_limit_bytes=4 * 1024 * 1024),
        cost_estimate=pl.CostEstimate(flops=1, bytes_accessed=10**6, transcendentals=0),
    )(*blocks.values())


def split_kernel(n_lo, choice_ref, *refs):
    pieces, (keep_ref, give_ref) = refs[:-2], refs[-2:]
    n_hi, held = pieces[0].shape[:2]
    my_y = lax.div(lax.axis_index("sec"), 2)
    my_op = lax.axis_index("op")
    for q, piece in enumerate(pieces):
        y = jnp.bitwise_xor(my_y, q // n_lo)
        choices = [choice_ref[t, y] for t in range(2)]
        for k in range(n_hi):
            o = jnp.bitwise_xor(my_op, k * n_lo + q % n_lo)
            for choice, out_ref in zip(choices, (keep_ref, give_ref)):
                block = piece[k, 0]
                for i in range(1, held):
                    block = jnp.where(choice == i, piece[k, i], block)
                out_ref[y, o] = block


def split(choice, pieces, n_lo):
    n_hi, held, rows, width = pieces[0].shape
    out = jax.ShapeDtypeStruct((choice.shape[1], n_hi * n_lo, rows, width), BF16)
    return pl.pallas_call(
        functools.partial(split_kernel, n_lo),
        out_shape=[out, out],
        in_specs=[VMEM] * (1 + len(pieces)),
        out_specs=[VMEM] * 2,
        compiler_params=pltpu.CompilerParams(vmem_limit_bytes=8 * 1024 * 1024),
        cost_estimate=pl.CostEstimate(flops=10**6, bytes_accessed=2 * 10**6, transcendentals=0),
    )(choice, *pieces)


def halves(left_ref, table_ref, half_ref):
    n_left, width = left_ref.shape[0], left_ref.shape[1]
    for s in range(table_ref.shape[0]):
        for l in range(0, n_left, 2):
            two = [jnp.dot(left_ref[l + i], table_ref[s], preferred_element_type=jnp.float32) for i in range(2)]
            p = s * n_left + l
            for m in range(width // CHUNK):
                piece = jnp.concatenate([x[m * CHUNK:(m + 1) * CHUNK, :] for x in two], axis=0)
                half_ref[m, p * CHUNK:(p + 2) * CHUNK, :] = piece.astype(BF16)


def first_halves(table, left):
    n_slot, width, _ = table.shape
    n_left = left.shape[0]
    return pl.pallas_call(
        halves,
        out_shape=jax.ShapeDtypeStruct((width // CHUNK, n_slot * n_left * CHUNK, width), BF16),
        in_specs=[VMEM] * 2,
        out_specs=VMEM,
        compiler_params=pltpu.CompilerParams(vmem_limit_bytes=8 * 1024 * 1024),
        cost_estimate=pl.CostEstimate(flops=2 * n_slot * n_left * width**3, bytes_accessed=10**6, transcendentals=0),
    )(left, table)


def terms_kernel(split_rows, left_ref, right_ref, weight_ref, first_ref, table_ref, out_ref, half_ref, sum_ref):
    width, n_right = left_ref.shape[1], right_ref.shape[0]
    held = sum_ref.shape[0] // width
    chunks = width // CHUNK
    halves(left_ref, table_ref, half_ref)

    for m in range(0, chunks, 2):
        two = [jnp.dot(weight_ref[...], jnp.concatenate([first_ref[m + i], half_ref[m + i]], axis=0),
                       preferred_element_type=jnp.float32) for i in range(2)]
        for j in range(held):
            for r in range(n_right):
                p = j * n_right + r
                piece = jnp.concatenate([x[p * CHUNK:(p + 1) * CHUNK, :] for x in two], axis=0)
                sum_ref[j * width + m * CHUNK:j * width + (m + 2) * CHUNK, r * width:(r + 1) * width] = piece.astype(BF16)

    for j in range(held):
        acc = None
        for r in range(n_right):
            part = lax.dot_general(
                sum_ref[j * width:(j + 1) * width, r * width:(r + 1) * width], right_ref[r], NT,
                preferred_element_type=jnp.float32)
            acc = part if acc is None else acc + part
        acc = acc.astype(out_ref.dtype)
        if split_rows:
            n_op, rows = out_ref.shape[0], out_ref.shape[2]
            for o in range(n_op):
                out_ref[o, j] = acc[o * rows:(o + 1) * rows, :]
        else:
            out_ref[j] = acc


def terms(first, table, left, right, weight, held, n_op):
    n_slot, width, _ = table.shape
    n_left, n_right = left.shape[0], right.shape[0]
    rows = width // n_op
    split_rows = rows % 16 == 0
    shape = (n_op, held, rows, width) if split_rows else (held, width, width)
    n_pair, n_cell = n_slot * n_left, held * n_right
    blocks = n_pair + n_cell + n_left + n_right + n_slot + 4 * held
    out = pl.pallas_call(
        functools.partial(terms_kernel, split_rows),
        out_shape=jax.ShapeDtypeStruct(shape, BF16),
        in_specs=[VMEM] * 5,
        out_specs=VMEM,
        scratch_shapes=[
            pltpu.VMEM((width // CHUNK, n_pair * CHUNK, width), BF16),
            pltpu.VMEM((held * width, n_right * width), BF16),
        ],
        compiler_params=pltpu.CompilerParams(vmem_limit_bytes=2 * width * width * blocks + 12 * 1024 * 1024),
        cost_estimate=pl.CostEstimate(flops=3 * 10**9, bytes_accessed=4 * 10**6, transcendentals=0),
    )(left, right, weight, first, table)
    if not split_rows:
        out = out.reshape(held, n_op, rows, width).transpose(1, 0, 2, 3)
    return out


def shards(psi, left_ops, right_ops, send_list, term_slot, term_out, left_pick, right_pick):
    held, rows, width = psi.shape
    n_sec, n_op = send_list.shape[:2]
    n_lo = 2
    n_hi, n_y = n_op // n_lo, n_sec // 2

    def swap(x, sec_bits, op_bits):
        pairs = [(s * n_op + o, (s ^ sec_bits) * n_op + (o ^ op_bits)) for s in range(n_sec) for o in range(n_op)]
        return lax.ppermute(x, ("sec", "op"), pairs)

    near = fetch(psi)
    mine = stack({0: near} | {k: swap(psi, 0, k * n_lo) for k in [n_hi - 1, *range(1, n_hi - 1)]})
    pieces = [mine] + [swap(mine, 2 * (q // n_lo), q % n_lo) for q in range(1, n_y * n_lo)]
    choice, weight = prepare(
        send_list, term_slot, term_out, left_pick, right_pick, held, rows, width, left_ops.shape[0], right_ops.shape[0])
    keep, give = (x.reshape(n_y, width, width) for x in split(choice, pieces, n_lo))
    got = swap(give, 1, 0)
    first = first_halves(keep, left_ops)
    partial_sum = terms(first, got, left_ops, right_ops, weight, held, n_op)
    parts = lax.all_to_all(partial_sum, "op", 0, 0, tiled=True)
    return jnp.sum(parts.astype(jnp.float32), axis=0)


def solution(mesh):
    in_specs = (
        P("sec", "op", None),
        P(("sec", "op"), None, None),
        P(("sec", "op"), None, None),
        P(),
        P(("sec", "op")),
        P(("sec", "op")),
        P(("sec", "op")),
        P(("sec", "op")),
    )
    out_specs = P("sec", "op", None)
    return jax.shard_map(shards, mesh=mesh, in_specs=in_specs, out_specs=out_specs, check_vma=False)
```

```python
import functools

import jax
import jax.numpy as jnp
from jax import lax
from jax.experimental import pallas as pl
from jax.experimental.pallas import tpu as pltpu
from jax.sharding import PartitionSpec as P

CHUNK = 8
VMEM = pl.BlockSpec(memory_space=pltpu.VMEM)
SMEM = pl.BlockSpec(memory_space=pltpu.SMEM)
ANY = pl.BlockSpec(memory_space=pl.ANY)
NT = (((1,), (1,)), ((), ()))
BF16 = jnp.bfloat16


def fetch_kernel(from_ref, to_ref, sem):
    copy = pltpu.make_async_copy(from_ref, to_ref, sem)
    copy.start()
    copy.wait()


def fetch(x):
    return pl.pallas_call(
        fetch_kernel,
        out_shape=jax.ShapeDtypeStruct(x.shape, x.dtype),
        in_specs=[ANY],
        out_specs=VMEM,
        scratch_shapes=[pltpu.SemaphoreType.DMA],
        compiler_params=pltpu.CompilerParams(vmem_limit_bytes=4 * 1024 * 1024),
        cost_estimate=pl.CostEstimate(flops=1, bytes_accessed=10**6, transcendentals=0),
    )(x)


def prepare_kernel(n_left, n_right, held, listed_ref, code_ref, choice_ref, weight_ref):
    n_pair, n_cell = weight_ref.shape[1] // CHUNK, weight_ref.shape[0] // CHUNK
    me, my_op = lax.axis_index("sec"), lax.axis_index("op")
    core = lax.rem(me, 2)
    for t in range(2):
        for y in range(choice_ref.shape[1]):
            source = 2 * y + core
            choice = listed_ref[source, jnp.bitwise_xor(me, t), 0, my_op] - source * held
            choice_ref[t, y] = jnp.full(choice_ref.shape[2:], choice.astype(jnp.float32)).astype(BF16)

    code = code_ref[...]
    cell, code = lax.rem(code, n_cell), lax.div(code, n_cell)
    left, slot = lax.rem(code, n_left), lax.div(code, n_left)
    other = jnp.bitwise_xor(lax.rem(slot, 2), core)
    pair = (other * (n_pair // (2 * n_left)) + lax.div(slot, 2)) * n_left + left
    n_term = cell.shape[1]
    row_cell = lax.broadcasted_iota(jnp.int32, (n_cell * CHUNK, n_term), 0) // CHUNK
    row_pair = lax.broadcasted_iota(jnp.int32, (n_pair * CHUNK, n_term), 0) // CHUNK
    in_cell = jnp.where(row_cell == cell, 1.0, 0.0).astype(BF16)
    in_pair = jnp.where(row_pair == pair, 1.0, 0.0).astype(BF16)
    count = lax.dot_general(in_cell, in_pair, NT, preferred_element_type=jnp.float32)
    a = lax.broadcasted_iota(jnp.int32, count.shape, 0) % CHUNK
    b = lax.broadcasted_iota(jnp.int32, count.shape, 1) % CHUNK
    weight_ref[...] = jnp.where(a == b, count, 0.0).astype(BF16)


def prepare(send_list, term_slot, term_out, left_pick, right_pick, held, rows, width, n_left, n_right):
    n_sec = send_list.shape[0]
    n_pair, n_cell = n_sec * n_left, held * n_right
    n_term = term_slot.shape[0]
    code = ((term_slot * n_left + left_pick) * held + term_out) * n_right + right_pick
    return pl.pallas_call(
        functools.partial(prepare_kernel, n_left, n_right, held),
        out_shape=[
            jax.ShapeDtypeStruct((2, n_sec // 2, rows, width), BF16),
            jax.ShapeDtypeStruct((n_cell * CHUNK, n_pair * CHUNK), BF16),
        ],
        in_specs=[SMEM, VMEM],
        out_specs=[VMEM] * 2,
        compiler_params=pltpu.CompilerParams(vmem_limit_bytes=8 * 1024 * 1024),
        cost_estimate=pl.CostEstimate(flops=10**9, bytes_accessed=4 * 10**6, transcendentals=0),
    )(send_list.transpose(0, 2, 3, 1), code.reshape(1, n_term))


def stack_kernel(order, *refs):
    for k, ref in zip(order, refs[:-1]):
        refs[-1][k] = ref[...]


def stack(blocks):
    first = next(iter(blocks.values()))
    return pl.pallas_call(
        functools.partial(stack_kernel, tuple(blocks)),
        out_shape=jax.ShapeDtypeStruct((len(blocks),) + first.shape, first.dtype),
        in_specs=[VMEM] * len(blocks),
        out_specs=VMEM,
        compiler_params=pltpu.CompilerParams(vmem_limit_bytes=4 * 1024 * 1024),
        cost_estimate=pl.CostEstimate(flops=1, bytes_accessed=10**6, transcendentals=0),
    )(*blocks.values())


def split_kernel(n_lo, choice_ref, *refs):
    pieces, (keep_ref, give_ref) = refs[:-2], refs[-2:]
    n_hi, held = pieces[0].shape[:2]
    my_y = lax.div(lax.axis_index("sec"), 2)
    my_op = lax.axis_index("op")
    for q, piece in enumerate(pieces):
        y = jnp.bitwise_xor(my_y, q // n_lo)
        choices = [choice_ref[t, y] for t in range(2)]
        for k in range(n_hi):
            o = jnp.bitwise_xor(my_op, k * n_lo + q % n_lo)
            for choice, out_ref in zip(choices, (keep_ref, give_ref)):
                block = piece[k, 0]
                for i in range(1, held):
                    block = jnp.where(choice == i, piece[k, i], block)
                out_ref[y, o] = block


def split(choice, pieces, n_lo):
    n_hi, held, rows, width = pieces[0].shape
    out = jax.ShapeDtypeStruct((choice.shape[1], n_hi * n_lo, rows, width), BF16)
    return pl.pallas_call(
        functools.partial(split_kernel, n_lo),
        out_shape=[out, out],
        in_specs=[VMEM] * (1 + len(pieces)),
        out_specs=[VMEM] * 2,
        compiler_params=pltpu.CompilerParams(vmem_limit_bytes=8 * 1024 * 1024),
        cost_estimate=pl.CostEstimate(flops=10**6, bytes_accessed=2 * 10**6, transcendentals=0),
    )(choice, *pieces)


def halves(left_ref, table_ref, half_ref):
    n_left, width = left_ref.shape[0], left_ref.shape[1]
    for s in range(table_ref.shape[0]):
        for l in range(0, n_left, 2):
            two = [jnp.dot(left_ref[l + i], table_ref[s], preferred_element_type=jnp.float32) for i in range(2)]
            p = s * n_left + l
            for m in range(width // CHUNK):
                piece = jnp.concatenate([x[m * CHUNK:(m + 1) * CHUNK, :] for x in two], axis=0)
                half_ref[m, p * CHUNK:(p + 2) * CHUNK, :] = piece.astype(BF16)


def first_halves(table, left):
    n_slot, width, _ = table.shape
    n_left = left.shape[0]
    return pl.pallas_call(
        halves,
        out_shape=jax.ShapeDtypeStruct((width // CHUNK, n_slot * n_left * CHUNK, width), BF16),
        in_specs=[VMEM] * 2,
        out_specs=VMEM,
        compiler_params=pltpu.CompilerParams(vmem_limit_bytes=8 * 1024 * 1024),
        cost_estimate=pl.CostEstimate(flops=2 * n_slot * n_left * width**3, bytes_accessed=10**6, transcendentals=0),
    )(left, table)


def terms_kernel(n_lo, left_ref, right_ref, weight_ref, first_ref, table_ref, *refs):
    outs, (half_ref, sum_ref, total_ref) = refs[:-3], refs[-3:]
    width, n_right = left_ref.shape[1], right_ref.shape[0]
    held = sum_ref.shape[0] // width
    chunks = width // CHUNK
    halves(left_ref, table_ref, half_ref)

    for m in range(0, chunks, 2):
        two = [jnp.dot(weight_ref[...], jnp.concatenate([first_ref[m + i], half_ref[m + i]], axis=0),
                       preferred_element_type=jnp.float32) for i in range(2)]
        for j in range(held):
            for r in range(n_right):
                p = j * n_right + r
                piece = jnp.concatenate([x[p * CHUNK:(p + 1) * CHUNK, :] for x in two], axis=0)
                sum_ref[j * width + m * CHUNK:j * width + (m + 2) * CHUNK, r * width:(r + 1) * width] = piece.astype(BF16)

    for j in range(held):
        acc = None
        for r in range(n_right):
            part = lax.dot_general(
                sum_ref[j * width:(j + 1) * width, r * width:(r + 1) * width], right_ref[r], NT,
                preferred_element_type=jnp.float32)
            acc = part if acc is None else acc + part
        total_ref[j] = acc
    if len(outs) == 1:
        outs[0][...] = total_ref[...]
        return
    half, _, rows, _ = outs[0].shape
    me = lax.axis_index("op")
    for p, out_ref in enumerate(outs):
        i, low = p // 2, half * (1 - p % 2)
        for k in range(half):
            start = pl.multiple_of(jnp.bitwise_xor(me, (low + k) * n_lo + i) * rows, rows)
            for j in range(held):
                out_ref[k, j] = total_ref[j, pl.ds(start, rows), :].astype(out_ref.dtype)


def terms(first, table, left, right, weight, held, n_op, n_lo):
    n_slot, width, _ = table.shape
    n_left, n_right = left.shape[0], right.shape[0]
    rows, n_hi = width // n_op, n_op // n_lo
    if rows % 16 == 0:
        shape = (n_hi // 2, held, rows, width)
        out_shape = [jax.ShapeDtypeStruct(shape, x) for x in (jnp.float32, jnp.float32, BF16, BF16)]
    else:
        out_shape = [jax.ShapeDtypeStruct((held, width, width), jnp.float32)]
    n_pair, n_cell = n_slot * n_left, held * n_right
    blocks = n_pair + n_cell + n_left + n_right + n_slot + 10 * held
    outs = pl.pallas_call(
        functools.partial(terms_kernel, n_lo),
        out_shape=out_shape,
        in_specs=[VMEM] * 5,
        out_specs=[VMEM] * len(out_shape),
        scratch_shapes=[
            pltpu.VMEM((width // CHUNK, n_pair * CHUNK, width), BF16),
            pltpu.VMEM((held * width, n_right * width), BF16),
            pltpu.VMEM((held, width, width), jnp.float32),
        ],
        compiler_params=pltpu.CompilerParams(vmem_limit_bytes=2 * width * width * blocks + 12 * 1024 * 1024),
        cost_estimate=pl.CostEstimate(flops=3 * 10**9, bytes_accessed=4 * 10**6, transcendentals=0),
    )(left, right, weight, first, table)
    if rows % 16:
        whole, me, half = outs[0].reshape(held, n_op, rows, width), lax.axis_index("op"), n_op // 2
        part = [lax.dynamic_index_in_dim(whole, me ^ o, axis=1, keepdims=False) for o in range(n_op)]
        outs = [jnp.stack(x) for x in (part[half::n_lo], part[:half:n_lo], part[half + 1::n_lo], part[1:half:n_lo])]
        outs = [x.astype(BF16) if i > 1 else x for i, x in enumerate(outs)]
    return outs


def combine_kernel(own_ref, other_ref, *outs):
    for k, out_ref in enumerate(outs):
        out_ref[...] = (own_ref[k] + other_ref[k].astype(jnp.float32)).astype(out_ref.dtype)


def combine(own, other, types):
    return pl.pallas_call(
        combine_kernel,
        out_shape=[jax.ShapeDtypeStruct(own.shape[1:], x) for x in types],
        in_specs=[VMEM] * 2,
        out_specs=[VMEM] * len(types),
        compiler_params=pltpu.CompilerParams(vmem_limit_bytes=8 * 1024 * 1024),
        cost_estimate=pl.CostEstimate(flops=10**6, bytes_accessed=10**6, transcendentals=0),
    )(own, other)


def shards(psi, left_ops, right_ops, send_list, term_slot, term_out, left_pick, right_pick):
    held, rows, width = psi.shape
    n_sec, n_op = send_list.shape[:2]
    n_lo = 2
    n_hi, n_y = n_op // n_lo, n_sec // 2

    def swap(x, sec_bits, op_bits):
        pairs = [(s * n_op + o, (s ^ sec_bits) * n_op + (o ^ op_bits)) for s in range(n_sec) for o in range(n_op)]
        return lax.ppermute(x, ("sec", "op"), pairs)

    near = fetch(psi)
    mine = stack({0: near} | {k: swap(psi, 0, k * n_lo) for k in [n_hi - 1, *range(1, n_hi - 1)]})
    pieces = [mine] + [swap(mine, 2 * (q // n_lo), q % n_lo) for q in range(1, n_y * n_lo)]
    choice, weight = prepare(
        send_list, term_slot, term_out, left_pick, right_pick, held, rows, width, left_ops.shape[0], right_ops.shape[0])
    keep, give = (x.reshape(n_y, width, width) for x in split(choice, pieces, n_lo))
    got = swap(give, 1, 0)
    first = first_halves(keep, left_ops)
    own_far, own_near, far, near = terms(first, got, left_ops, right_ops, weight, held, n_op, n_lo)
    half = n_hi // 2
    far = combine(own_far, swap(far, 0, 1), [BF16] * half)
    near = combine(own_near, swap(near, 0, 1), [jnp.float32] + [BF16] * (half - 1))
    parts = near + far
    total = swap(parts[n_hi - 1], 0, (n_hi - 1) * n_lo).astype(jnp.float32)
    for k in range(n_hi - 2, 0, -1):
        total = total + swap(parts[k], 0, k * n_lo).astype(jnp.float32)
    return total + parts[0]


def solution(mesh):
    in_specs = (
        P("sec", "op", None),
        P(("sec", "op"), None, None),
        P(("sec", "op"), None, None),
        P(),
        P(("sec", "op")),
        P(("sec", "op")),
        P(("sec", "op")),
        P(("sec", "op")),
    )
    out_specs = P("sec", "op", None)
    return jax.shard_map(shards, mesh=mesh, in_specs=in_specs, out_specs=out_specs, check_vma=False)
```

```python
import functools

import jax
import jax.numpy as jnp
from jax import lax
from jax.experimental import pallas as pl
from jax.experimental.pallas import tpu as pltpu
from jax.sharding import PartitionSpec as P

CHUNK = 8
VMEM = pl.BlockSpec(memory_space=pltpu.VMEM)
SMEM = pl.BlockSpec(memory_space=pltpu.SMEM)
ANY = pl.BlockSpec(memory_space=pl.ANY)
NT = (((1,), (1,)), ((), ()))
BF16 = jnp.bfloat16


def fetch_kernel(from_ref, to_ref, sem):
    copy = pltpu.make_async_copy(from_ref, to_ref, sem)
    copy.start()
    copy.wait()


def fetch(x):
    return pl.pallas_call(
        fetch_kernel,
        out_shape=jax.ShapeDtypeStruct(x.shape, x.dtype),
        in_specs=[ANY],
        out_specs=VMEM,
        scratch_shapes=[pltpu.SemaphoreType.DMA],
        compiler_params=pltpu.CompilerParams(vmem_limit_bytes=4 * 1024 * 1024),
        cost_estimate=pl.CostEstimate(flops=1, bytes_accessed=10**6, transcendentals=0),
    )(x)


def prepare_kernel(n_left, n_right, held, listed_ref, code_ref, choice_ref, weight_ref):
    n_pair, n_cell = weight_ref.shape[1] // CHUNK, weight_ref.shape[0] // CHUNK
    me, my_op = lax.axis_index("sec"), lax.axis_index("op")
    core = lax.rem(me, 2)
    for t in range(2):
        for y in range(choice_ref.shape[1]):
            source = 2 * y + core
            choice = listed_ref[source, jnp.bitwise_xor(me, t), 0, my_op] - source * held
            choice_ref[t, y] = jnp.full(choice_ref.shape[2:], choice.astype(jnp.float32)).astype(BF16)

    code = code_ref[...]
    cell, code = lax.rem(code, n_cell), lax.div(code, n_cell)
    left, slot = lax.rem(code, n_left), lax.div(code, n_left)
    other = jnp.bitwise_xor(lax.rem(slot, 2), core)
    pair = (other * (n_pair // (2 * n_left)) + lax.div(slot, 2)) * n_left + left
    n_term = cell.shape[1]
    row_cell = lax.broadcasted_iota(jnp.int32, (n_cell * CHUNK, n_term), 0) // CHUNK
    row_pair = lax.broadcasted_iota(jnp.int32, (n_pair * CHUNK, n_term), 0) // CHUNK
    in_cell = jnp.where(row_cell == cell, 1.0, 0.0).astype(BF16)
    in_pair = jnp.where(row_pair == pair, 1.0, 0.0).astype(BF16)
    count = lax.dot_general(in_cell, in_pair, NT, preferred_element_type=jnp.float32)
    a = lax.broadcasted_iota(jnp.int32, count.shape, 0) % CHUNK
    b = lax.broadcasted_iota(jnp.int32, count.shape, 1) % CHUNK
    weight_ref[...] = jnp.where(a == b, count, 0.0).astype(BF16)


def prepare(send_list, term_slot, term_out, left_pick, right_pick, held, rows, width, n_left, n_right):
    n_sec = send_list.shape[0]
    n_pair, n_cell = n_sec * n_left, held * n_right
    n_term = term_slot.shape[0]
    code = ((term_slot * n_left + left_pick) * held + term_out) * n_right + right_pick
    return pl.pallas_call(
        functools.partial(prepare_kernel, n_left, n_right, held),
        out_shape=[
            jax.ShapeDtypeStruct((2, n_sec // 2, rows, width), BF16),
            jax.ShapeDtypeStruct((n_cell * CHUNK, n_pair * CHUNK), BF16),
        ],
        in_specs=[SMEM, VMEM],
        out_specs=[VMEM] * 2,
        compiler_params=pltpu.CompilerParams(vmem_limit_bytes=8 * 1024 * 1024),
        cost_estimate=pl.CostEstimate(flops=10**9, bytes_accessed=4 * 10**6, transcendentals=0),
    )(send_list.transpose(0, 2, 3, 1), code.reshape(1, n_term))


def stack_kernel(order, *refs):
    for k, ref in zip(order, refs[:-1]):
        refs[-1][k] = ref[...]


def stack(blocks):
    first = next(iter(blocks.values()))
    return pl.pallas_call(
        functools.partial(stack_kernel, tuple(blocks)),
        out_shape=jax.ShapeDtypeStruct((len(blocks),) + first.shape, first.dtype),
        in_specs=[VMEM] * len(blocks),
        out_specs=VMEM,
        compiler_params=pltpu.CompilerParams(vmem_limit_bytes=4 * 1024 * 1024),
        cost_estimate=pl.CostEstimate(flops=1, bytes_accessed=10**6, transcendentals=0),
    )(*blocks.values())


def split_kernel(n_lo, choice_ref, *refs):
    pieces, (keep_ref, give_ref) = refs[:-2], refs[-2:]
    n_hi, held = pieces[0].shape[:2]
    my_y = lax.div(lax.axis_index("sec"), 2)
    my_op = lax.axis_index("op")
    for q, piece in enumerate(pieces):
        y = jnp.bitwise_xor(my_y, q // n_lo)
        choices = [choice_ref[t, y] for t in range(2)]
        for k in range(n_hi):
            o = jnp.bitwise_xor(my_op, k * n_lo + q % n_lo)
            for choice, out_ref in zip(choices, (keep_ref, give_ref)):
                block = piece[k, 0]
                for i in range(1, held):
                    block = jnp.where(choice == i, piece[k, i], block)
                out_ref[y, o] = block


def split(choice, pieces, n_lo):
    n_hi, held, rows, width = pieces[0].shape
    out = jax.ShapeDtypeStruct((choice.shape[1], n_hi * n_lo, rows, width), BF16)
    return pl.pallas_call(
        functools.partial(split_kernel, n_lo),
        out_shape=[out, out],
        in_specs=[VMEM] * (1 + len(pieces)),
        out_specs=[VMEM] * 2,
        compiler_params=pltpu.CompilerParams(vmem_limit_bytes=8 * 1024 * 1024),
        cost_estimate=pl.CostEstimate(flops=10**6, bytes_accessed=2 * 10**6, transcendentals=0),
    )(choice, *pieces)


def halves(left_ref, table_ref, half_ref):
    n_left, width = left_ref.shape[0], left_ref.shape[1]
    for s in range(table_ref.shape[0]):
        for l in range(0, n_left, 2):
            two = [jnp.dot(left_ref[l + i], table_ref[s], preferred_element_type=jnp.float32) for i in range(2)]
            p = s * n_left + l
            for m in range(width // CHUNK):
                piece = jnp.concatenate([x[m * CHUNK:(m + 1) * CHUNK, :] for x in two], axis=0)
                half_ref[m, p * CHUNK:(p + 2) * CHUNK, :] = piece.astype(BF16)


def first_halves(table, left):
    n_slot, width, _ = table.shape
    n_left = left.shape[0]
    return pl.pallas_call(
        halves,
        out_shape=jax.ShapeDtypeStruct((width // CHUNK, n_slot * n_left * CHUNK, width), BF16),
        in_specs=[VMEM] * 2,
        out_specs=VMEM,
        compiler_params=pltpu.CompilerParams(vmem_limit_bytes=8 * 1024 * 1024),
        cost_estimate=pl.CostEstimate(flops=2 * n_slot * n_left * width**3, bytes_accessed=10**6, transcendentals=0),
    )(left, table)


def terms_kernel(n_lo, keys, left_ref, right_ref, weight_ref, first_ref, table_ref, *refs):
    outs, (half_ref, sum_ref, total_ref) = refs[:-3], refs[-3:]
    width, n_right = left_ref.shape[1], right_ref.shape[0]
    held = sum_ref.shape[0] // width
    chunks = width // CHUNK
    halves(left_ref, table_ref, half_ref)

    for m in range(0, chunks, 2):
        two = [jnp.dot(weight_ref[...], jnp.concatenate([first_ref[m + i], half_ref[m + i]], axis=0),
                       preferred_element_type=jnp.float32) for i in range(2)]
        for j in range(held):
            for r in range(n_right):
                p = j * n_right + r
                piece = jnp.concatenate([x[p * CHUNK:(p + 1) * CHUNK, :] for x in two], axis=0)
                sum_ref[j * width + m * CHUNK:j * width + (m + 2) * CHUNK, r * width:(r + 1) * width] = piece.astype(BF16)

    for j in range(held):
        acc = None
        for r in range(n_right):
            part = lax.dot_general(
                sum_ref[j * width:(j + 1) * width, r * width:(r + 1) * width], right_ref[r], NT,
                preferred_element_type=jnp.float32)
            acc = part if acc is None else acc + part
        total_ref[j] = acc
    if not keys:
        outs[0][...] = total_ref[...]
        return
    me = lax.axis_index("op")
    for (k, i), (out_ref, place) in zip(keys, [(x, p) for x in outs for p in range(x.shape[0])]):
        rows = out_ref.shape[2]
        start = pl.multiple_of(jnp.bitwise_xor(me, k * n_lo + i) * rows, rows)
        for j in range(held):
            out_ref[place, j] = total_ref[j, pl.ds(start, rows), :].astype(out_ref.dtype)


def terms(first, table, left, right, weight, held, n_op, n_lo, staged, direct):
    n_slot, width, _ = table.shape
    n_left, n_right = left.shape[0], right.shape[0]
    rows, n_hi = width // n_op, n_op // n_lo
    groups = [[(k, i) for k in staged] for i in range(n_lo)] + [[(direct, i)] for i in range(n_lo)]
    types = [BF16 if p else jnp.float32 for p in range(len(groups))]
    if rows % 16 == 0:
        keys = sum(groups, [])
        out_shape = [jax.ShapeDtypeStruct((len(group), held, rows, width), x) for group, x in zip(groups, types)]
    else:
        keys = []
        out_shape = [jax.ShapeDtypeStruct((held, width, width), jnp.float32)]
    n_pair, n_cell = n_slot * n_left, held * n_right
    blocks = n_pair + n_cell + n_left + n_right + n_slot + 10 * held
    outs = pl.pallas_call(
        functools.partial(terms_kernel, n_lo, keys),
        out_shape=out_shape,
        in_specs=[VMEM] * 5,
        out_specs=[VMEM] * len(out_shape),
        scratch_shapes=[
            pltpu.VMEM((width // CHUNK, n_pair * CHUNK, width), BF16),
            pltpu.VMEM((held * width, n_right * width), BF16),
            pltpu.VMEM((held, width, width), jnp.float32),
        ],
        compiler_params=pltpu.CompilerParams(vmem_limit_bytes=2 * width * width * blocks + 12 * 1024 * 1024),
        cost_estimate=pl.CostEstimate(flops=3 * 10**9, bytes_accessed=4 * 10**6, transcendentals=0),
    )(left, right, weight, first, table)
    if not keys:
        whole, me = outs[0].reshape(held, n_op, rows, width), lax.axis_index("op")
        part = [lax.dynamic_index_in_dim(whole, me ^ o, axis=1, keepdims=False) for o in range(n_op)]
        outs = [jnp.stack([part[k * n_lo + i] for k, i in group]).astype(x) for group, x in zip(groups, types)]
    return outs


def combine_kernel(own_ref, other_ref, *outs):
    for k, out_ref in enumerate(outs, start=1):
        out_ref[...] = (own_ref[k] + other_ref[k].astype(jnp.float32)).astype(BF16)


def combine(own, other):
    return pl.pallas_call(
        combine_kernel,
        out_shape=[jax.ShapeDtypeStruct(own.shape[1:], BF16)] * (own.shape[0] - 1),
        in_specs=[VMEM] * 2,
        out_specs=[VMEM] * (own.shape[0] - 1),
        compiler_params=pltpu.CompilerParams(vmem_limit_bytes=4 * 1024 * 1024),
        cost_estimate=pl.CostEstimate(flops=10**6, bytes_accessed=10**6, transcendentals=0),
    )(own, other)


def shards(psi, left_ops, right_ops, send_list, term_slot, term_out, left_pick, right_pick):
    held, rows, width = psi.shape
    n_sec, n_op = send_list.shape[:2]
    n_lo = 2
    n_hi, n_y = n_op // n_lo, n_sec // 2

    def swap(x, sec_bits, op_bits):
        pairs = [(s * n_op + o, (s ^ sec_bits) * n_op + (o ^ op_bits)) for s in range(n_sec) for o in range(n_op)]
        return lax.ppermute(x, ("sec", "op"), pairs)

    near = fetch(psi)
    mine = stack({0: near} | {k: swap(psi, 0, k * n_lo) for k in [n_hi - 1, *range(1, n_hi - 1)]})
    pieces = [mine] + [swap(mine, 2 * (q // n_lo), q % n_lo) for q in range(1, n_y * n_lo)]
    choice, weight = prepare(
        send_list, term_slot, term_out, left_pick, right_pick, held, rows, width, left_ops.shape[0], right_ops.shape[0])
    keep, give = (x.reshape(n_y, width, width) for x in split(choice, pieces, n_lo))
    got = swap(give, 1, 0)
    first = first_halves(keep, left_ops)
    direct = n_hi - 1
    staged = [k for k in range(n_hi) if k != direct]
    own, other, *far = terms(first, got, left_ops, right_ops, weight, held, n_op, n_lo, staged, direct)
    total = None
    for i in range(n_lo - 1, -1, -1):
        part = swap(far[i][0], 0, direct * n_lo + i).astype(jnp.float32)
        total = part if total is None else total + part
    other = swap(other, 0, 1)
    sums = dict(zip(staged[1:], combine(own, other)))
    for k in staged[1:]:
        total = total + swap(sums[k], 0, k * n_lo).astype(jnp.float32)
    return total + own[0] + other[0].astype(jnp.float32)


def solution(mesh):
    in_specs = (
        P("sec", "op", None),
        P(("sec", "op"), None, None),
        P(("sec", "op"), None, None),
        P(),
        P(("sec", "op")),
        P(("sec", "op")),
        P(("sec", "op")),
        P(("sec", "op")),
    )
    out_specs = P("sec", "op", None)
    return jax.shard_map(shards, mesh=mesh, in_specs=in_specs, out_specs=out_specs, check_vma=False)
```

```python
import functools

import jax
import jax.numpy as jnp
from jax import lax
from jax.experimental import pallas as pl
from jax.experimental.pallas import tpu as pltpu
from jax.sharding import PartitionSpec as P

CHUNK = 8
VMEM = pl.BlockSpec(memory_space=pltpu.VMEM)
SMEM = pl.BlockSpec(memory_space=pltpu.SMEM)
ANY = pl.BlockSpec(memory_space=pl.ANY)
NT = (((1,), (1,)), ((), ()))
BF16 = jnp.bfloat16


def fetch_kernel(from_ref, to_ref, sem):
    copy = pltpu.make_async_copy(from_ref, to_ref, sem)
    copy.start()
    copy.wait()


def fetch(x):
    return pl.pallas_call(
        fetch_kernel,
        out_shape=jax.ShapeDtypeStruct(x.shape, x.dtype),
        in_specs=[ANY],
        out_specs=VMEM,
        scratch_shapes=[pltpu.SemaphoreType.DMA],
        compiler_params=pltpu.CompilerParams(vmem_limit_bytes=4 * 1024 * 1024),
        cost_estimate=pl.CostEstimate(flops=1, bytes_accessed=10**6, transcendentals=0),
    )(x)


def prepare_kernel(n_left, n_right, held, listed_ref, code_ref, choice_ref, weight_ref):
    n_pair, n_cell = weight_ref.shape[1] // CHUNK, weight_ref.shape[0] // CHUNK
    me, my_op = lax.axis_index("sec"), lax.axis_index("op")
    for t in range(2):
        for y in range(choice_ref.shape[1]):
            source = jnp.bitwise_xor(me, 2 * y)
            choice = listed_ref[source, jnp.bitwise_xor(me, t), 0, my_op] - source * held
            choice_ref[t, y] = jnp.full(choice_ref.shape[2:], choice.astype(jnp.float32)).astype(BF16)

    code = code_ref[...]
    cell, code = lax.rem(code, n_cell), lax.div(code, n_cell)
    left, slot = lax.rem(code, n_left), lax.div(code, n_left)
    slot = jnp.bitwise_xor(slot, me)
    pair = (lax.rem(slot, 2) * (n_pair // (2 * n_left)) + lax.div(slot, 2)) * n_left + left
    n_term = cell.shape[1]
    row_cell = lax.broadcasted_iota(jnp.int32, (n_cell * CHUNK, n_term), 0) // CHUNK
    row_pair = lax.broadcasted_iota(jnp.int32, (n_pair * CHUNK, n_term), 0) // CHUNK
    in_cell = jnp.where(row_cell == cell, 1.0, 0.0).astype(BF16)
    in_pair = jnp.where(row_pair == pair, 1.0, 0.0).astype(BF16)
    count = lax.dot_general(in_cell, in_pair, NT, preferred_element_type=jnp.float32)
    a = lax.broadcasted_iota(jnp.int32, count.shape, 0) % CHUNK
    b = lax.broadcasted_iota(jnp.int32, count.shape, 1) % CHUNK
    weight_ref[...] = jnp.where(a == b, count, 0.0).astype(BF16)


def prepare(send_list, term_slot, term_out, left_pick, right_pick, held, rows, width, n_left, n_right):
    n_sec = send_list.shape[0]
    n_pair, n_cell = n_sec * n_left, held * n_right
    n_term = term_slot.shape[0]
    code = ((term_slot * n_left + left_pick) * held + term_out) * n_right + right_pick
    return pl.pallas_call(
        functools.partial(prepare_kernel, n_left, n_right, held),
        out_shape=[
            jax.ShapeDtypeStruct((2, n_sec // 2, rows, width), BF16),
            jax.ShapeDtypeStruct((n_cell * CHUNK, n_pair * CHUNK), BF16),
        ],
        in_specs=[SMEM, VMEM],
        out_specs=[VMEM] * 2,
        compiler_params=pltpu.CompilerParams(vmem_limit_bytes=8 * 1024 * 1024),
        cost_estimate=pl.CostEstimate(flops=10**9, bytes_accessed=4 * 10**6, transcendentals=0),
    )(send_list.transpose(0, 2, 3, 1), code.reshape(1, n_term))


def stack_kernel(order, *refs):
    for k, ref in zip(order, refs[:-1]):
        refs[-1][k] = ref[...]


def stack(blocks):
    first = next(iter(blocks.values()))
    return pl.pallas_call(
        functools.partial(stack_kernel, tuple(blocks)),
        out_shape=jax.ShapeDtypeStruct((len(blocks),) + first.shape, first.dtype),
        in_specs=[VMEM] * len(blocks),
        out_specs=VMEM,
        compiler_params=pltpu.CompilerParams(vmem_limit_bytes=4 * 1024 * 1024),
        cost_estimate=pl.CostEstimate(flops=1, bytes_accessed=10**6, transcendentals=0),
    )(*blocks.values())


def split_kernel(n_lo, choice_ref, *refs):
    pieces, (keep_ref, first_ref, rest_ref) = refs[:-3], refs[-3:]
    n_hi, held = pieces[0].shape[:2]
    my_op = lax.axis_index("op")
    for q, piece in enumerate(pieces):
        y = q // n_lo
        choices = [choice_ref[t, y] for t in range(2)]
        give = (first_ref, 0) if y == 0 else (rest_ref, y - 1)
        for k in range(n_hi):
            o = jnp.bitwise_xor(my_op, k * n_lo + q % n_lo)
            for choice, (out_ref, place) in zip(choices, ((keep_ref, y), give)):
                block = piece[k, 0]
                for i in range(1, held):
                    block = jnp.where(choice == i, piece[k, i], block)
                out_ref[place, o] = block


def split(choice, pieces, n_lo):
    n_hi, held, rows, width = pieces[0].shape
    n_y = choice.shape[1]
    outs = pl.pallas_call(
        functools.partial(split_kernel, n_lo),
        out_shape=[jax.ShapeDtypeStruct((y, n_hi * n_lo, rows, width), BF16) for y in (n_y, 1, n_y - 1)],
        in_specs=[VMEM] * (1 + len(pieces)),
        out_specs=[VMEM] * 3,
        compiler_params=pltpu.CompilerParams(vmem_limit_bytes=8 * 1024 * 1024),
        cost_estimate=pl.CostEstimate(flops=10**6, bytes_accessed=2 * 10**6, transcendentals=0),
    )(choice, *pieces)
    return [x.reshape(x.shape[0], width, width) for x in outs]


def halves(left_ref, table_ref, half_ref):
    n_left, width = left_ref.shape[0], left_ref.shape[1]
    for s in range(table_ref.shape[0]):
        for l in range(0, n_left, 2):
            two = [jnp.dot(left_ref[l + i], table_ref[s], preferred_element_type=jnp.float32) for i in range(2)]
            p = s * n_left + l
            for m in range(width // CHUNK):
                piece = jnp.concatenate([x[m * CHUNK:(m + 1) * CHUNK, :] for x in two], axis=0)
                half_ref[m, p * CHUNK:(p + 2) * CHUNK, :] = piece.astype(BF16)


def first_halves(table, left):
    n_slot, width, _ = table.shape
    n_left = left.shape[0]
    return pl.pallas_call(
        halves,
        out_shape=jax.ShapeDtypeStruct((width // CHUNK, n_slot * n_left * CHUNK, width), BF16),
        in_specs=[VMEM] * 2,
        out_specs=VMEM,
        compiler_params=pltpu.CompilerParams(vmem_limit_bytes=8 * 1024 * 1024),
        cost_estimate=pl.CostEstimate(flops=2 * n_slot * n_left * width**3, bytes_accessed=10**6, transcendentals=0),
    )(left, table)


def terms_kernel(n_lo, keys, left_ref, right_ref, weight_ref, first_ref, second_ref, table_ref, *refs):
    outs, (half_ref, sum_ref, total_ref) = refs[:-3], refs[-3:]
    width, n_right = left_ref.shape[1], right_ref.shape[0]
    held = sum_ref.shape[0] // width
    chunks = width // CHUNK
    halves(left_ref, table_ref, half_ref)

    for m in range(0, chunks, 2):
        two = [jnp.dot(weight_ref[...], jnp.concatenate([x[m + i] for x in (first_ref, second_ref, half_ref)], axis=0),
                       preferred_element_type=jnp.float32) for i in range(2)]
        for j in range(held):
            for r in range(n_right):
                p = j * n_right + r
                piece = jnp.concatenate([x[p * CHUNK:(p + 1) * CHUNK, :] for x in two], axis=0)
                sum_ref[j * width + m * CHUNK:j * width + (m + 2) * CHUNK, r * width:(r + 1) * width] = piece.astype(BF16)

    for j in range(held):
        acc = None
        for r in range(n_right):
            part = lax.dot_general(
                sum_ref[j * width:(j + 1) * width, r * width:(r + 1) * width], right_ref[r], NT,
                preferred_element_type=jnp.float32)
            acc = part if acc is None else acc + part
        total_ref[j] = acc
    if not keys:
        outs[0][...] = total_ref[...]
        return
    me = lax.axis_index("op")
    core = lax.rem(lax.axis_index("sec"), 2)
    for (even, odd, i), (out_ref, place) in zip(keys, [(x, p) for x in outs for p in range(x.shape[0])]):
        rows = out_ref.shape[2]
        k = jnp.where(core == 0, even, odd)
        start = pl.multiple_of(jnp.bitwise_xor(me, k * n_lo + i) * rows, rows)
        for j in range(held):
            out_ref[place, j] = total_ref[j, pl.ds(start, rows), :].astype(out_ref.dtype)


def terms(first, second, table, left, right, weight, held, n_op, n_lo, staged, direct):
    n_slot, width, _ = table.shape
    n_left, n_right = left.shape[0], right.shape[0]
    rows, n_hi = width // n_op, n_op // n_lo
    groups = [[(*k, i) for k in staged] for i in range(n_lo)] + [[(*direct, i)] for i in range(n_lo)]
    types = [BF16 if p else jnp.float32 for p in range(len(groups))]
    if rows % 16 == 0:
        keys = sum(groups, [])
        out_shape = [jax.ShapeDtypeStruct((len(group), held, rows, width), x) for group, x in zip(groups, types)]
    else:
        keys = []
        out_shape = [jax.ShapeDtypeStruct((held, width, width), jnp.float32)]
    n_pair, n_cell = n_slot * n_left, held * n_right
    blocks = n_pair + n_cell + n_left + n_right + n_slot + 10 * held
    outs = pl.pallas_call(
        functools.partial(terms_kernel, n_lo, keys),
        out_shape=out_shape,
        in_specs=[VMEM] * 6,
        out_specs=[VMEM] * len(out_shape),
        scratch_shapes=[
            pltpu.VMEM((width // CHUNK, n_pair * CHUNK, width), BF16),
            pltpu.VMEM((held * width, n_right * width), BF16),
            pltpu.VMEM((held, width, width), jnp.float32),
        ],
        compiler_params=pltpu.CompilerParams(vmem_limit_bytes=2 * width * width * blocks + 12 * 1024 * 1024),
        cost_estimate=pl.CostEstimate(flops=3 * 10**9, bytes_accessed=4 * 10**6, transcendentals=0),
    )(left, right, weight, first, second, table)
    if not keys:
        whole, me = outs[0].reshape(held, n_op, rows, width), lax.axis_index("op")
        core = lax.rem(lax.axis_index("sec"), 2)

        def part(even, odd, i):
            o = me ^ (jnp.where(core == 0, even, odd) * n_lo + i)
            return lax.dynamic_index_in_dim(whole, o, axis=1, keepdims=False)

        outs = [jnp.stack([part(*key) for key in group]).astype(x) for group, x in zip(groups, types)]
    return outs


def combine_kernel(own_ref, other_ref, *outs):
    for k, out_ref in enumerate(outs, start=1):
        out_ref[...] = (own_ref[k] + other_ref[k].astype(jnp.float32)).astype(BF16)


def combine(own, other):
    return pl.pallas_call(
        combine_kernel,
        out_shape=[jax.ShapeDtypeStruct(own.shape[1:], BF16)] * (own.shape[0] - 1),
        in_specs=[VMEM] * 2,
        out_specs=[VMEM] * (own.shape[0] - 1),
        compiler_params=pltpu.CompilerParams(vmem_limit_bytes=4 * 1024 * 1024),
        cost_estimate=pl.CostEstimate(flops=10**6, bytes_accessed=10**6, transcendentals=0),
    )(own, other)


def shards(psi, left_ops, right_ops, send_list, term_slot, term_out, left_pick, right_pick):
    held, rows, width = psi.shape
    n_sec, n_op = send_list.shape[:2]
    n_lo = 2
    n_hi, n_y = n_op // n_lo, n_sec // 2

    def swap(x, sec_bits, op_bits):
        pairs = [(s * n_op + o, (s ^ sec_bits) * n_op + (o ^ op_bits)) for s in range(n_sec) for o in range(n_op)]
        return lax.ppermute(x, ("sec", "op"), pairs)

    near = fetch(psi)
    mine = stack({0: near} | {k: swap(psi, 0, k * n_lo) for k in [n_hi - 1, *range(1, n_hi - 1)]})
    pieces = [mine] + [swap(mine, 2 * (q // n_lo), q % n_lo) for q in range(1, n_y * n_lo)]
    choice, weight = prepare(
        send_list, term_slot, term_out, left_pick, right_pick, held, rows, width, left_ops.shape[0], right_ops.shape[0])
    keep, *give = split(choice, pieces, n_lo)
    got = [swap(x, 1, 0) for x in give]
    first, second = first_halves(keep, left_ops), first_halves(got[0], left_ops)
    def meet(x, k, i):
        pairs = [(s * n_op + o, s * n_op + (o ^ (k[s % 2] * n_lo + i))) for s in range(n_sec) for o in range(n_op)]
        return lax.ppermute(x, ("sec", "op"), pairs)

    direct = (n_hi - 1, 1)
    staged = list(zip(range(n_hi - 1), [0, *range(n_hi - 1, 1, -1)]))
    own, other, *far = terms(first, second, got[1], left_ops, right_ops, weight, held, n_op, n_lo, staged, direct)
    total = None
    for i in range(n_lo - 1, -1, -1):
        part = meet(far[i][0], direct, i).astype(jnp.float32)
        total = part if total is None else total + part
    other = swap(other, 0, 1)
    for k, part in zip(staged[1:], combine(own, other)):
        total = total + meet(part, k, 0).astype(jnp.float32)
    return total + own[0] + other[0].astype(jnp.float32)


def solution(mesh):
    in_specs = (
        P("sec", "op", None),
        P(("sec", "op"), None, None),
        P(("sec", "op"), None, None),
        P(),
        P(("sec", "op")),
        P(("sec", "op")),
        P(("sec", "op")),
        P(("sec", "op")),
    )
    out_specs = P("sec", "op", None)
    return jax.shard_map(shards, mesh=mesh, in_specs=in_specs, out_specs=out_specs, check_vma=False)
```

```python
import functools

import jax
import jax.numpy as jnp
from jax import lax
from jax.experimental import pallas as pl
from jax.experimental.pallas import tpu as pltpu
from jax.sharding import PartitionSpec as P

CHUNK = 8
VMEM = pl.BlockSpec(memory_space=pltpu.VMEM)
SMEM = pl.BlockSpec(memory_space=pltpu.SMEM)
ANY = pl.BlockSpec(memory_space=pl.ANY)
NT = (((1,), (1,)), ((), ()))
BF16 = jnp.bfloat16


def fetch_kernel(from_ref, to_ref, sem):
    copy = pltpu.make_async_copy(from_ref, to_ref, sem)
    copy.start()
    copy.wait()


def fetch(x):
    return pl.pallas_call(
        fetch_kernel,
        out_shape=jax.ShapeDtypeStruct(x.shape, x.dtype),
        in_specs=[ANY],
        out_specs=VMEM,
        scratch_shapes=[pltpu.SemaphoreType.DMA],
        compiler_params=pltpu.CompilerParams(vmem_limit_bytes=4 * 1024 * 1024),
        cost_estimate=pl.CostEstimate(flops=1, bytes_accessed=10**6, transcendentals=0),
    )(x)


def prepare_kernel(n_left, n_right, held, listed_ref, code_ref, choice_ref, weight_ref):
    n_pair, n_cell = weight_ref.shape[1] // CHUNK, weight_ref.shape[0] // CHUNK
    me, my_op = lax.axis_index("sec"), lax.axis_index("op")
    core = lax.rem(me, 2)
    for t in range(2):
        for y in range(choice_ref.shape[1]):
            source = 2 * y + core
            choice = listed_ref[source, jnp.bitwise_xor(me, t), 0, my_op] - source * held
            choice_ref[t, y] = jnp.full(choice_ref.shape[2:], choice.astype(jnp.float32)).astype(BF16)

    code = code_ref[...]
    cell, code = lax.rem(code, n_cell), lax.div(code, n_cell)
    left, slot = lax.rem(code, n_left), lax.div(code, n_left)
    other = jnp.bitwise_xor(lax.rem(slot, 2), core)
    pair = (other * (n_pair // (2 * n_left)) + lax.div(slot, 2)) * n_left + left
    n_term = cell.shape[1]
    row_cell = lax.broadcasted_iota(jnp.int32, (n_cell * CHUNK, n_term), 0) // CHUNK
    row_pair = lax.broadcasted_iota(jnp.int32, (n_pair * CHUNK, n_term), 0) // CHUNK
    in_cell = jnp.where(row_cell == cell, 1.0, 0.0).astype(BF16)
    in_pair = jnp.where(row_pair == pair, 1.0, 0.0).astype(BF16)
    count = lax.dot_general(in_cell, in_pair, NT, preferred_element_type=jnp.float32)
    a = lax.broadcasted_iota(jnp.int32, count.shape, 0) % CHUNK
    b = lax.broadcasted_iota(jnp.int32, count.shape, 1) % CHUNK
    weight_ref[...] = jnp.where(a == b, count, 0.0).astype(BF16)


def prepare(send_list, term_slot, term_out, left_pick, right_pick, held, rows, width, n_left, n_right):
    n_sec = send_list.shape[0]
    n_pair, n_cell = n_sec * n_left, held * n_right
    n_term = term_slot.shape[0]
    code = ((term_slot * n_left + left_pick) * held + term_out) * n_right + right_pick
    return pl.pallas_call(
        functools.partial(prepare_kernel, n_left, n_right, held),
        out_shape=[
            jax.ShapeDtypeStruct((2, n_sec // 2, rows, width), BF16),
            jax.ShapeDtypeStruct((n_cell * CHUNK, n_pair * CHUNK), BF16),
        ],
        in_specs=[SMEM, VMEM],
        out_specs=[VMEM] * 2,
        compiler_params=pltpu.CompilerParams(vmem_limit_bytes=8 * 1024 * 1024),
        cost_estimate=pl.CostEstimate(flops=10**9, bytes_accessed=4 * 10**6, transcendentals=0),
    )(send_list.transpose(0, 2, 3, 1), code.reshape(1, n_term))


def stack_kernel(order, *refs):
    for k, ref in zip(order, refs[:-1]):
        refs[-1][k] = ref[...]


def stack(blocks):
    first = next(iter(blocks.values()))
    return pl.pallas_call(
        functools.partial(stack_kernel, tuple(blocks)),
        out_shape=jax.ShapeDtypeStruct((len(blocks),) + first.shape, first.dtype),
        in_specs=[VMEM] * len(blocks),
        out_specs=VMEM,
        compiler_params=pltpu.CompilerParams(vmem_limit_bytes=4 * 1024 * 1024),
        cost_estimate=pl.CostEstimate(flops=1, bytes_accessed=10**6, transcendentals=0),
    )(*blocks.values())


def split_kernel(n_lo, choice_ref, *refs):
    pieces, (keep_ref, give_ref) = refs[:-2], refs[-2:]
    n_hi, held = pieces[0].shape[:2]
    my_y = lax.div(lax.axis_index("sec"), 2)
    my_op = lax.axis_index("op")
    for q, piece in enumerate(pieces):
        y = jnp.bitwise_xor(my_y, q // n_lo)
        choices = [choice_ref[t, y] for t in range(2)]
        for k in range(n_hi):
            o = jnp.bitwise_xor(my_op, k * n_lo + q % n_lo)
            for choice, out_ref in zip(choices, (keep_ref, give_ref)):
                block = piece[k, 0]
                for i in range(1, held):
                    block = jnp.where(choice == i, piece[k, i], block)
                out_ref[y, o] = block


def split(choice, pieces, n_lo):
    n_hi, held, rows, width = pieces[0].shape
    out = jax.ShapeDtypeStruct((choice.shape[1], n_hi * n_lo, rows, width), BF16)
    return pl.pallas_call(
        functools.partial(split_kernel, n_lo),
        out_shape=[out, out],
        in_specs=[VMEM] * (1 + len(pieces)),
        out_specs=[VMEM] * 2,
        compiler_params=pltpu.CompilerParams(vmem_limit_bytes=8 * 1024 * 1024),
        cost_estimate=pl.CostEstimate(flops=10**6, bytes_accessed=2 * 10**6, transcendentals=0),
    )(choice, *pieces)


def halves(left_ref, table_ref, half_ref):
    n_left, width = left_ref.shape[0], left_ref.shape[1]
    for s in range(table_ref.shape[0]):
        for l in range(0, n_left, 2):
            two = [jnp.dot(left_ref[l + i], table_ref[s], preferred_element_type=jnp.float32) for i in range(2)]
            p = s * n_left + l
            for m in range(width // CHUNK):
                piece = jnp.concatenate([x[m * CHUNK:(m + 1) * CHUNK, :] for x in two], axis=0)
                half_ref[m, p * CHUNK:(p + 2) * CHUNK, :] = piece.astype(BF16)


def first_halves(table, left):
    n_slot, width, _ = table.shape
    n_left = left.shape[0]
    return pl.pallas_call(
        halves,
        out_shape=jax.ShapeDtypeStruct((width // CHUNK, n_slot * n_left * CHUNK, width), BF16),
        in_specs=[VMEM] * 2,
        out_specs=VMEM,
        compiler_params=pltpu.CompilerParams(vmem_limit_bytes=8 * 1024 * 1024),
        cost_estimate=pl.CostEstimate(flops=2 * n_slot * n_left * width**3, bytes_accessed=10**6, transcendentals=0),
    )(left, table)


def terms_kernel(n_lo, keys, left_ref, right_ref, weight_ref, first_ref, table_ref, *refs):
    outs, (half_ref, sum_ref, total_ref) = refs[:-3], refs[-3:]
    width, n_right = left_ref.shape[1], right_ref.shape[0]
    held = sum_ref.shape[0] // width
    chunks = width // CHUNK
    halves(left_ref, table_ref, half_ref)

    for m in range(0, chunks, 2):
        two = [jnp.dot(weight_ref[...], jnp.concatenate([first_ref[m + i], half_ref[m + i]], axis=0),
                       preferred_element_type=jnp.float32) for i in range(2)]
        for j in range(held):
            for r in range(n_right):
                p = j * n_right + r
                piece = jnp.concatenate([x[p * CHUNK:(p + 1) * CHUNK, :] for x in two], axis=0)
                sum_ref[j * width + m * CHUNK:j * width + (m + 2) * CHUNK, r * width:(r + 1) * width] = piece.astype(BF16)

    for j in range(held):
        acc = None
        for r in range(n_right):
            part = lax.dot_general(
                sum_ref[j * width:(j + 1) * width, r * width:(r + 1) * width], right_ref[r], NT,
                preferred_element_type=jnp.float32)
            acc = part if acc is None else acc + part
        total_ref[j] = acc
    if not keys:
        outs[0][...] = total_ref[...]
        return
    me = lax.axis_index("op")
    core = lax.rem(lax.axis_index("sec"), 2)
    for (even, odd, i), (out_ref, place) in zip(keys, [(x, p) for x in outs for p in range(x.shape[0])]):
        rows = out_ref.shape[2]
        k = jnp.where(core == 0, even, odd)
        start = pl.multiple_of(jnp.bitwise_xor(me, k * n_lo + i) * rows, rows)
        for j in range(held):
            out_ref[place, j] = total_ref[j, pl.ds(start, rows), :].astype(out_ref.dtype)


def terms(first, table, left, right, weight, held, n_op, n_lo, staged, direct):
    n_slot, width, _ = table.shape
    n_left, n_right = left.shape[0], right.shape[0]
    rows, n_hi = width // n_op, n_op // n_lo
    groups = [[(*k, i) for k in staged] for i in range(n_lo)] + [[(*direct, i)] for i in range(n_lo)]
    types = [BF16 if p else jnp.float32 for p in range(len(groups))]
    if rows % 16 == 0:
        keys = sum(groups, [])
        out_shape = [jax.ShapeDtypeStruct((len(group), held, rows, width), x) for group, x in zip(groups, types)]
    else:
        keys = []
        out_shape = [jax.ShapeDtypeStruct((held, width, width), jnp.float32)]
    n_pair, n_cell = n_slot * n_left, held * n_right
    blocks = n_pair + n_cell + n_left + n_right + n_slot + 10 * held
    outs = pl.pallas_call(
        functools.partial(terms_kernel, n_lo, keys),
        out_shape=out_shape,
        in_specs=[VMEM] * 5,
        out_specs=[VMEM] * len(out_shape),
        scratch_shapes=[
            pltpu.VMEM((width // CHUNK, n_pair * CHUNK, width), BF16),
            pltpu.VMEM((held * width, n_right * width), BF16),
            pltpu.VMEM((held, width, width), jnp.float32),
        ],
        compiler_params=pltpu.CompilerParams(vmem_limit_bytes=2 * width * width * blocks + 12 * 1024 * 1024),
        cost_estimate=pl.CostEstimate(flops=3 * 10**9, bytes_accessed=4 * 10**6, transcendentals=0),
    )(left, right, weight, first, table)
    if not keys:
        whole, me = outs[0].reshape(held, n_op, rows, width), lax.axis_index("op")
        core = lax.rem(lax.axis_index("sec"), 2)

        def part(even, odd, i):
            o = me ^ (jnp.where(core == 0, even, odd) * n_lo + i)
            return lax.dynamic_index_in_dim(whole, o, axis=1, keepdims=False)

        outs = [jnp.stack([part(*key) for key in group]).astype(x) for group, x in zip(groups, types)]
    return outs


def combine_kernel(own_ref, other_ref, *outs):
    for k, out_ref in enumerate(outs, start=1):
        out_ref[...] = (own_ref[k] + other_ref[k].astype(jnp.float32)).astype(BF16)


def combine(own, other):
    return pl.pallas_call(
        combine_kernel,
        out_shape=[jax.ShapeDtypeStruct(own.shape[1:], BF16)] * (own.shape[0] - 1),
        in_specs=[VMEM] * 2,
        out_specs=[VMEM] * (own.shape[0] - 1),
        compiler_params=pltpu.CompilerParams(vmem_limit_bytes=4 * 1024 * 1024),
        cost_estimate=pl.CostEstimate(flops=10**6, bytes_accessed=10**6, transcendentals=0),
    )(own, other)


def shards(psi, left_ops, right_ops, send_list, term_slot, term_out, left_pick, right_pick):
    held, rows, width = psi.shape
    n_sec, n_op = send_list.shape[:2]
    n_lo = 2
    n_hi, n_y = n_op // n_lo, n_sec // 2

    def swap(x, sec_bits, op_bits):
        pairs = [(s * n_op + o, (s ^ sec_bits) * n_op + (o ^ op_bits)) for s in range(n_sec) for o in range(n_op)]
        return lax.ppermute(x, ("sec", "op"), pairs)

    near = fetch(psi)
    mine = stack({0: near} | {k: swap(psi, 0, k * n_lo) for k in [n_hi - 1, *range(1, n_hi - 1)]})
    pieces = [mine] + [swap(mine, 2 * (q // n_lo), q % n_lo) for q in range(1, n_y * n_lo)]
    choice, weight = prepare(
        send_list, term_slot, term_out, left_pick, right_pick, held, rows, width, left_ops.shape[0], right_ops.shape[0])
    keep, give = (x.reshape(n_y, width, width) for x in split(choice, pieces, n_lo))
    got = swap(give, 1, 0)
    first = first_halves(keep, left_ops)
    def meet(x, k, i):
        pairs = [(s * n_op + o, s * n_op + (o ^ (k[s % 2] * n_lo + i))) for s in range(n_sec) for o in range(n_op)]
        return lax.ppermute(x, ("sec", "op"), pairs)

    direct = (n_hi - 1, 1)
    staged = list(zip(range(n_hi - 1), [0, *range(n_hi - 1, 1, -1)]))
    own, other, *far = terms(first, got, left_ops, right_ops, weight, held, n_op, n_lo, staged, direct)
    total = None
    for i in range(n_lo - 1, -1, -1):
        part = meet(far[i][0], direct, i).astype(jnp.float32)
        total = part if total is None else total + part
    other = swap(other, 0, 1)
    for k, part in zip(staged[1:], combine(own, other)):
        total = total + meet(part, k, 0).astype(jnp.float32)
    return total + own[0] + other[0].astype(jnp.float32)


def solution(mesh):
    in_specs = (
        P("sec", "op", None),
        P(("sec", "op"), None, None),
        P(("sec", "op"), None, None),
        P(),
        P(("sec", "op")),
        P(("sec", "op")),
        P(("sec", "op")),
        P(("sec", "op")),
    )
    out_specs = P("sec", "op", None)
    return jax.shard_map(shards, mesh=mesh, in_specs=in_specs, out_specs=out_specs, check_vma=False)
```

```python
import functools

import jax
import jax.numpy as jnp
from jax import lax
from jax.experimental import pallas as pl
from jax.experimental.pallas import tpu as pltpu
from jax.sharding import PartitionSpec as P

CHUNK = 8
VMEM = pl.BlockSpec(memory_space=pltpu.VMEM)
SMEM = pl.BlockSpec(memory_space=pltpu.SMEM)
ANY = pl.BlockSpec(memory_space=pl.ANY)
NT = (((1,), (1,)), ((), ()))
BF16 = jnp.bfloat16


def fetch_kernel(from_ref, to_ref, sem):
    copy = pltpu.make_async_copy(from_ref, to_ref, sem)
    copy.start()
    copy.wait()


def fetch(x):
    return pl.pallas_call(
        fetch_kernel,
        out_shape=jax.ShapeDtypeStruct(x.shape, x.dtype),
        in_specs=[ANY],
        out_specs=VMEM,
        scratch_shapes=[pltpu.SemaphoreType.DMA],
        compiler_params=pltpu.CompilerParams(vmem_limit_bytes=4 * 1024 * 1024),
        cost_estimate=pl.CostEstimate(flops=1, bytes_accessed=10**6, transcendentals=0),
    )(x)


def prepare_kernel(n_left, n_right, held, listed_ref, code_ref, choice_ref, weight_ref):
    n_pair, n_cell = weight_ref.shape[1] // CHUNK, weight_ref.shape[0] // CHUNK
    me, my_op = lax.axis_index("sec"), lax.axis_index("op")
    core = lax.rem(me, 2)
    for t in range(2):
        for y in range(choice_ref.shape[1]):
            source = 2 * y + core
            choice = listed_ref[source, jnp.bitwise_xor(me, t), 0, my_op] - source * held
            choice_ref[t, y] = jnp.full(choice_ref.shape[2:], choice.astype(jnp.float32)).astype(BF16)

    code = code_ref[...]
    cell, code = lax.rem(code, n_cell), lax.div(code, n_cell)
    left, slot = lax.rem(code, n_left), lax.div(code, n_left)
    other = jnp.bitwise_xor(lax.rem(slot, 2), core)
    pair = (other * (n_pair // (2 * n_left)) + lax.div(slot, 2)) * n_left + left
    n_term = cell.shape[1]
    row_cell = lax.broadcasted_iota(jnp.int32, (n_cell * CHUNK, n_term), 0) // CHUNK
    row_pair = lax.broadcasted_iota(jnp.int32, (n_pair * CHUNK, n_term), 0) // CHUNK
    in_cell = jnp.where(row_cell == cell, 1.0, 0.0).astype(BF16)
    in_pair = jnp.where(row_pair == pair, 1.0, 0.0).astype(BF16)
    count = lax.dot_general(in_cell, in_pair, NT, preferred_element_type=jnp.float32)
    a = lax.broadcasted_iota(jnp.int32, count.shape, 0) % CHUNK
    b = lax.broadcasted_iota(jnp.int32, count.shape, 1) % CHUNK
    weight_ref[...] = jnp.where(a == b, count, 0.0).astype(BF16)


def prepare(send_list, term_slot, term_out, left_pick, right_pick, held, rows, width, n_left, n_right):
    n_sec = send_list.shape[0]
    n_pair, n_cell = n_sec * n_left, held * n_right
    n_term = term_slot.shape[0]
    code = ((term_slot * n_left + left_pick) * held + term_out) * n_right + right_pick
    return pl.pallas_call(
        functools.partial(prepare_kernel, n_left, n_right, held),
        out_shape=[
            jax.ShapeDtypeStruct((2, n_sec // 2, rows, width), BF16),
            jax.ShapeDtypeStruct((n_cell * CHUNK, n_pair * CHUNK), BF16),
        ],
        in_specs=[SMEM, VMEM],
        out_specs=[VMEM] * 2,
        compiler_params=pltpu.CompilerParams(vmem_limit_bytes=8 * 1024 * 1024),
        cost_estimate=pl.CostEstimate(flops=10**9, bytes_accessed=4 * 10**6, transcendentals=0),
    )(send_list.transpose(0, 2, 3, 1), code.reshape(1, n_term))


def stack_kernel(order, *refs):
    for k, ref in zip(order, refs[:-1]):
        refs[-1][k] = ref[...]


def stack(blocks):
    first = next(iter(blocks.values()))
    return pl.pallas_call(
        functools.partial(stack_kernel, tuple(blocks)),
        out_shape=jax.ShapeDtypeStruct((len(blocks),) + first.shape, first.dtype),
        in_specs=[VMEM] * len(blocks),
        out_specs=VMEM,
        compiler_params=pltpu.CompilerParams(vmem_limit_bytes=4 * 1024 * 1024),
        cost_estimate=pl.CostEstimate(flops=1, bytes_accessed=10**6, transcendentals=0),
    )(*blocks.values())


def split_kernel(n_lo, choice_ref, *refs):
    pieces, (keep_ref, give_ref) = refs[:-2], refs[-2:]
    n_hi, held = pieces[0].shape[:2]
    my_y = lax.div(lax.axis_index("sec"), 2)
    my_op = lax.axis_index("op")
    for q, piece in enumerate(pieces):
        y = jnp.bitwise_xor(my_y, q // n_lo)
        choices = [choice_ref[t, y] for t in range(2)]
        for k in range(n_hi):
            o = jnp.bitwise_xor(my_op, k * n_lo + q % n_lo)
            for choice, out_ref in zip(choices, (keep_ref, give_ref)):
                block = piece[k, 0]
                for i in range(1, held):
                    block = jnp.where(choice == i, piece[k, i], block)
                out_ref[y, o] = block


def split(choice, pieces, n_lo):
    n_hi, held, rows, width = pieces[0].shape
    out = jax.ShapeDtypeStruct((choice.shape[1], n_hi * n_lo, rows, width), BF16)
    return pl.pallas_call(
        functools.partial(split_kernel, n_lo),
        out_shape=[out, out],
        in_specs=[VMEM] * (1 + len(pieces)),
        out_specs=[VMEM] * 2,
        compiler_params=pltpu.CompilerParams(vmem_limit_bytes=8 * 1024 * 1024),
        cost_estimate=pl.CostEstimate(flops=10**6, bytes_accessed=2 * 10**6, transcendentals=0),
    )(choice, *pieces)


def halves(left_ref, table_ref, half_ref):
    n_left, width = left_ref.shape[0], left_ref.shape[1]
    for s in range(table_ref.shape[0]):
        for l in range(0, n_left, 2):
            two = [jnp.dot(left_ref[l + i], table_ref[s], preferred_element_type=jnp.float32) for i in range(2)]
            p = s * n_left + l
            for m in range(width // CHUNK):
                piece = jnp.concatenate([x[m * CHUNK:(m + 1) * CHUNK, :] for x in two], axis=0)
                half_ref[m, p * CHUNK:(p + 2) * CHUNK, :] = piece.astype(BF16)


def first_halves(table, left):
    n_slot, width, _ = table.shape
    n_left = left.shape[0]
    return pl.pallas_call(
        halves,
        out_shape=jax.ShapeDtypeStruct((width // CHUNK, n_slot * n_left * CHUNK, width), BF16),
        in_specs=[VMEM] * 2,
        out_specs=VMEM,
        compiler_params=pltpu.CompilerParams(vmem_limit_bytes=8 * 1024 * 1024),
        cost_estimate=pl.CostEstimate(flops=2 * n_slot * n_left * width**3, bytes_accessed=10**6, transcendentals=0),
    )(left, table)


def terms_kernel(n_lo, direct, keys, left_ref, right_ref, weight_ref, first_ref, table_ref, *refs):
    outs, (half_ref, sum_ref, total_ref) = refs[:-3], refs[-3:]
    width, n_right = left_ref.shape[1], right_ref.shape[0]
    held = sum_ref.shape[0] // width
    chunks = width // CHUNK
    halves(left_ref, table_ref, half_ref)

    for m in range(0, chunks, 2):
        two = [jnp.dot(weight_ref[...], jnp.concatenate([first_ref[m + i], half_ref[m + i]], axis=0),
                       preferred_element_type=jnp.float32) for i in range(2)]
        for j in range(held):
            for r in range(n_right):
                p = j * n_right + r
                piece = jnp.concatenate([x[p * CHUNK:(p + 1) * CHUNK, :] for x in two], axis=0)
                sum_ref[j * width + m * CHUNK:j * width + (m + 2) * CHUNK, r * width:(r + 1) * width] = piece.astype(BF16)

    for j in range(held):
        acc = None
        for r in range(n_right):
            part = lax.dot_general(
                sum_ref[j * width:(j + 1) * width, r * width:(r + 1) * width], right_ref[r], NT,
                preferred_element_type=jnp.float32)
            acc = part if acc is None else acc + part
        total_ref[j] = acc
    if not keys:
        outs[0][...] = total_ref[...]
        return
    me, core = lax.axis_index("op"), lax.rem(lax.axis_index("sec"), 2)
    for (k, i), (out_ref, place) in zip(keys, [(x, p) for x in outs for p in range(x.shape[0])]):
        rows = out_ref.shape[2]
        if k == direct:
            i = jnp.where(core == 0, i, n_lo - 1 - i)
        start = pl.multiple_of(jnp.bitwise_xor(me, k * n_lo + i) * rows, rows)
        for j in range(held):
            out_ref[place, j] = total_ref[j, pl.ds(start, rows), :].astype(out_ref.dtype)


def terms(first, table, left, right, weight, held, n_op, n_lo, staged, direct):
    n_slot, width, _ = table.shape
    n_left, n_right = left.shape[0], right.shape[0]
    rows, n_hi = width // n_op, n_op // n_lo
    groups = [[(k, i) for k in staged] for i in range(n_lo)] + [[(direct, i)] for i in range(n_lo)]
    types = [BF16 if p else jnp.float32 for p in range(len(groups))]
    if rows % 16 == 0:
        keys = sum(groups, [])
        out_shape = [jax.ShapeDtypeStruct((len(group), held, rows, width), x) for group, x in zip(groups, types)]
    else:
        keys = []
        out_shape = [jax.ShapeDtypeStruct((held, width, width), jnp.float32)]
    n_pair, n_cell = n_slot * n_left, held * n_right
    blocks = n_pair + n_cell + n_left + n_right + n_slot + 10 * held
    outs = pl.pallas_call(
        functools.partial(terms_kernel, n_lo, direct, keys),
        out_shape=out_shape,
        in_specs=[VMEM] * 5,
        out_specs=[VMEM] * len(out_shape),
        scratch_shapes=[
            pltpu.VMEM((width // CHUNK, n_pair * CHUNK, width), BF16),
            pltpu.VMEM((held * width, n_right * width), BF16),
            pltpu.VMEM((held, width, width), jnp.float32),
        ],
        compiler_params=pltpu.CompilerParams(vmem_limit_bytes=2 * width * width * blocks + 12 * 1024 * 1024),
        cost_estimate=pl.CostEstimate(flops=3 * 10**9, bytes_accessed=4 * 10**6, transcendentals=0),
    )(left, right, weight, first, table)
    if not keys:
        whole, me = outs[0].reshape(held, n_op, rows, width), lax.axis_index("op")
        part = [lax.dynamic_index_in_dim(whole, me ^ o, axis=1, keepdims=False) for o in range(n_op)]
        outs = [jnp.stack([part[k * n_lo + i] for k, i in group]).astype(x) for group, x in zip(groups, types)]
    return outs


def combine_kernel(own_ref, other_ref, *outs):
    for k, out_ref in enumerate(outs, start=1):
        out_ref[...] = (own_ref[k] + other_ref[k].astype(jnp.float32)).astype(BF16)


def combine(own, other):
    return pl.pallas_call(
        combine_kernel,
        out_shape=[jax.ShapeDtypeStruct(own.shape[1:], BF16)] * (own.shape[0] - 1),
        in_specs=[VMEM] * 2,
        out_specs=[VMEM] * (own.shape[0] - 1),
        compiler_params=pltpu.CompilerParams(vmem_limit_bytes=4 * 1024 * 1024),
        cost_estimate=pl.CostEstimate(flops=10**6, bytes_accessed=10**6, transcendentals=0),
    )(own, other)


def shards(psi, left_ops, right_ops, send_list, term_slot, term_out, left_pick, right_pick):
    held, rows, width = psi.shape
    n_sec, n_op = send_list.shape[:2]
    n_lo = 2
    n_hi, n_y = n_op // n_lo, n_sec // 2

    def swap(x, sec_bits, op_bits):
        pairs = [(s * n_op + o, (s ^ sec_bits) * n_op + (o ^ op_bits)) for s in range(n_sec) for o in range(n_op)]
        return lax.ppermute(x, ("sec", "op"), pairs)

    near = fetch(psi)
    mine = stack({0: near} | {k: swap(psi, 0, k * n_lo) for k in [n_hi - 1, *range(1, n_hi - 1)]})
    pieces = [mine] + [swap(mine, 2 * (q // n_lo), q % n_lo) for q in range(1, n_y * n_lo)]
    choice, weight = prepare(
        send_list, term_slot, term_out, left_pick, right_pick, held, rows, width, left_ops.shape[0], right_ops.shape[0])
    keep, give = (x.reshape(n_y, width, width) for x in split(choice, pieces, n_lo))
    got = swap(give, 1, 0)
    first = first_halves(keep, left_ops)
    direct = n_hi - 1
    staged = [k for k in range(n_hi) if k != direct]
    own, other, *far = terms(first, got, left_ops, right_ops, weight, held, n_op, n_lo, staged, direct)
    def meet(x, even, odd):
        bits = [even, odd]
        pairs = [(s * n_op + o, s * n_op + (o ^ bits[s % 2])) for s in range(n_sec) for o in range(n_op)]
        return lax.ppermute(x, ("sec", "op"), pairs)

    total = None
    for i in range(n_lo - 1, -1, -1):
        part = meet(far[i][0], direct * n_lo + i, direct * n_lo + (n_lo - 1 - i)).astype(jnp.float32)
        total = part if total is None else total + part
    other = swap(other, 0, 1)
    sums = dict(zip(staged[1:], combine(own, other)))
    for k in staged[1:]:
        total = total + swap(sums[k], 0, k * n_lo).astype(jnp.float32)
    return total + own[0] + other[0].astype(jnp.float32)


def solution(mesh):
    in_specs = (
        P("sec", "op", None),
        P(("sec", "op"), None, None),
        P(("sec", "op"), None, None),
        P(),
        P(("sec", "op")),
        P(("sec", "op")),
        P(("sec", "op")),
        P(("sec", "op")),
    )
    out_specs = P("sec", "op", None)
    return jax.shard_map(shards, mesh=mesh, in_specs=in_specs, out_specs=out_specs, check_vma=False)
```
